32 devices in a mesh: lon: 8 (over z, core), lat: 4 (over y, x).
Axes of the slice: x: 2, y: 2, z: 4, core: 2. Of those that a mesh axis runs over, the one named last changes fastest.
Arguments:
- land_sea: int32 [512, 1792], P('lat', 'lon'), may hold values from 0 to 1, as said below
- obs_cell: int32 [4, 8, 2048], P('lat', 'lon'), may hold values from 0 to 28671
- obs_value: float32 [4, 8, 2048], P('lat', 'lon'), may hold values from -12 to 12
- obs_weight: float32 [4, 8, 2048], P('lat', 'lon'), may hold values from 0.5 to 4
- intersection: int32 [4, 8], P('lat', 'lon'), may hold values from 1 to 16, as said below
- factors: float32 [40, 16, 16, 2048], P('lat', None, None, 'lon'), may hold values from -1 to 1, as said below
- coarse_inverse: float32 [512, 512], P(('lon', 'lat')), may hold values from -1 to 1, as said below
Outputs:
- solution: float32 [512, 1792], P('lat', 'lon')
- residual: float32 [512, 1792], P('lat', 'lon')
- preconditioned: float32 [512, 1792], P('lat', 'lon')
The draws below stay inside these ranges and needn't reach their ends.
Inputs may be any that keep to these rules, and one draw needn't show every extreme that they name: `land_sea`: 1 marks ocean and 0 land; the first and last rows of the grid are land. Some tile has intersection 16. `factors`: each block is lower triangular (zero where the third index exceeds the second) with a positive diagonal. `coarse_inverse`: symmetric and positive definite.
All inputs are finite; a program needn't handle non-finite values.
Results may differ from the reference program's by a relative error of at most 0.00012.
Values sent between devices are 32-bit elements; how exact they have to be, the bound alone decides.
A program may use at most 64 MiB of HBM per device.

```python
import math
import jax
import jax.numpy as jnp
from jax import lax

CY = 128
CX = 224
HW = 16
BS = 16
SUB = 4
OBS_DEV = 2048
ITERS = 1
LAT_TILES = 4
LON_TILES = 8
GRID_LAT = 512
GRID_LON = 1792
LAT_EXT = 160
LON_EXT = 256
NBLK = 10
COARSE_ALL = 512
N_LON = 8
N_LAT = 4


def draw_land_sea(key, part):
    key_block, key_cell = jax.random.split(jax.random.fold_in(key, 11))
    block_draw = jax.random.randint(key_block, (GRID_LAT // 4 + 1, GRID_LON // 4 + 1), 0, 100)
    block_land = jnp.repeat(jnp.repeat(block_draw < 28, 4, axis=0), 4, axis=1)[:GRID_LAT, :GRID_LON]
    cell_land = jax.random.randint(key_cell, (GRID_LAT, GRID_LON), 0, 100) < 6
    row_index = jnp.arange(GRID_LAT, dtype=jnp.int32)[:, None]
    polar = (row_index == 0) | (row_index == GRID_LAT - 1)
    land_cells = block_land | cell_land | polar
    return jnp.where(land_cells, 0, 1).astype(jnp.int32)


def draw_intersection(key, part):
    widths = jax.random.randint(jax.random.fold_in(key, 12), (LAT_TILES, LON_TILES), 1, HW + 1)
    first = (jnp.arange(LAT_TILES)[:, None] == 0) & (jnp.arange(LON_TILES)[None, :] == 0)
    return jnp.where(first, HW, widths).astype(jnp.int32)


def draw_obs_value(key, part):
    shape = (LAT_TILES, LON_TILES, OBS_DEV)
    lat_scale = 1.0 + 2.0 * jnp.arange(LAT_TILES, dtype=jnp.float32)[:, None, None] / max(LAT_TILES - 1, 1)
    lon_scale = 1.0 + 0.5 * jnp.arange(LON_TILES, dtype=jnp.float32)[None, :, None] / max(LON_TILES - 1, 1)
    inner_key = jax.random.fold_in(key, 13)
    base = jnp.clip(jax.random.normal(inner_key, shape, jnp.float32), -2.5, 2.5)
    return (base * lat_scale * lon_scale).astype(jnp.float32)


def draw_factors(key, part):
    shape = (LAT_TILES * NBLK, BS, BS, LON_TILES * LON_EXT)
    diag_shape = (LAT_TILES * NBLK, BS, 1, LON_TILES * LON_EXT)
    key_off, key_diag = jax.random.split(jax.random.fold_in(key, 14))
    off_diag = jnp.clip(0.12 * jax.random.normal(key_off, shape, jnp.float32), -0.3, 0.3)
    diagonal = jnp.exp(jax.random.uniform(key_diag, diag_shape, jnp.float32, math.log(0.3), math.log(0.8)))
    first_index = jnp.arange(BS)[:, None]
    second_index = jnp.arange(BS)[None, :]
    below = (second_index < first_index)[None, :, :, None]
    on_diag = (second_index == first_index)[None, :, :, None]
    return jnp.where(on_diag, diagonal, jnp.where(below, off_diag, 0.0)).astype(jnp.float32)


def draw_coarse_inverse(key, part):
    count = COARSE_ALL
    scale = 2.0 / (CY // SUB * (CX // SUB))
    key_noise, key_diag = jax.random.split(jax.random.fold_in(key, 15))
    noise = jnp.clip(jax.random.normal(key_noise, (count, count), jnp.float32), -5.0, 5.0)
    symmetric = (noise + noise.T) * (0.45 / math.sqrt(2.0 * count))
    diagonal = jnp.exp(jax.random.uniform(key_diag, (count,), jnp.float32, math.log(1.2), math.log(3.6)))
    return ((symmetric + jnp.diag(diagonal)) * scale).astype(jnp.float32)


def with_ends(entries, stream_key, smallest, high):
    longest = entries.shape.index(max(entries.shape))
    spots = []
    for shift in (0, 1):
        where = [jax.random.randint(jax.random.fold_in(stream_key, axis), (), 0, length) for axis, length in enumerate(entries.shape)]
        where[longest] = (where[longest] + shift) % entries.shape[longest]
        spots.append(tuple(where))
    return entries.at[spots[0]].set(smallest).at[spots[1]].set(high)


def steps_of(own_key, extent, cuts, least, top_value):
    gain, own = 1.0, jax.random.fold_in(own_key, 6)
    for position, shards_of in cuts:
        steps = jnp.exp(jax.random.uniform(jax.random.fold_in(own, position), (shards_of,), jnp.float32, least / len(cuts), top_value / len(cuts)))
        gain = gain * jnp.repeat(steps, extent[position] // shards_of).reshape([-1 if axis == position else 1 for axis in range(len(extent))])
    return gain


def setup_inputs(seed: int = 0) -> dict:
    streams_of = jax.random.split(jax.random.key(seed), 8)
    land_sea = draw_land_sea(jax.random.fold_in(streams_of[7], 71), 0)
    obs_cell = with_ends(jax.random.randint(streams_of[1], (LAT_TILES, LON_TILES, OBS_DEV), 0, CY * CX), jax.random.fold_in(streams_of[1], 1), 0, (CY * CX) - 1).astype(jnp.int32)
    obs_value = draw_obs_value(jax.random.fold_in(streams_of[7], 71), 0)
    obs_weight = jnp.clip(jnp.exp(math.log(4.0) - 2.0794415 * jax.random.uniform(streams_of[3], (LAT_TILES, LON_TILES, OBS_DEV), jnp.float32) ** steps_of(streams_of[3], (LAT_TILES, LON_TILES, OBS_DEV), ((0, 4), (1, 8)), -0.2, 0.2)), 0.5, 4.0)
    intersection = draw_intersection(jax.random.fold_in(streams_of[7], 71), 0)
    factors = draw_factors(jax.random.fold_in(streams_of[7], 71), 0)
    coarse_inverse = draw_coarse_inverse(jax.random.fold_in(streams_of[7], 71), 0)
    return dict(land_sea=land_sea, obs_cell=obs_cell, obs_value=obs_value, obs_weight=obs_weight, intersection=intersection, factors=factors, coarse_inverse=coarse_inverse)


DAMPING = 0.02


def wrap_pad(field, width):
    padded = jnp.pad(field, ((width, width), (0, 0)))
    return jnp.concatenate([padded[:, -width:], padded, padded[:, :width]], axis=1)


def tile_grid(per_tile):
    shaped = per_tile.reshape(N_LAT, N_LON, CY, CX)
    return jnp.transpose(shaped, (0, 2, 1, 3)).reshape(N_LAT * CY, N_LON * CX)


def operate(field, ocean, obs_diag, conduct):
    padded = wrap_pad(field, 1)
    east, west, north, south = conduct
    beside = east * padded[1:-1, 2:] + west * padded[1:-1, :-2] + north * padded[:-2, 1:-1] + south * padded[2:, 1:-1]
    coupling = (east + west + north + south) * field - beside
    return ocean * ((obs_diag + DAMPING) * field + coupling) + (1.0 - ocean) * field


def to_tiles(field):
    padded = wrap_pad(field, HW)
    upper = padded[:N_LAT * CY].reshape(N_LAT, CY, -1)[:, :2 * HW]
    lower = padded[2 * HW:].reshape(N_LAT, CY, -1)
    banded = jnp.concatenate([upper, lower], axis=1)
    left = banded[:, :, :N_LON * CX].reshape(N_LAT, LAT_EXT, N_LON, CX)[..., :2 * HW]
    right = banded[:, :, 2 * HW:].reshape(N_LAT, LAT_EXT, N_LON, CX)
    return jnp.concatenate([left, right], axis=3)


def from_tiles(contrib):
    upper = jnp.pad(contrib[:, :2 * HW], ((0, 0), (0, CY - 2 * HW), (0, 0), (0, 0)))
    upper = upper.reshape(N_LAT * CY, N_LON, LON_EXT)
    lower = contrib[:, 2 * HW:].reshape(N_LAT * CY, N_LON, LON_EXT)
    summed = jnp.pad(lower, ((2 * HW, 0), (0, 0), (0, 0))) + jnp.pad(upper, ((0, 2 * HW), (0, 0), (0, 0)))
    summed = summed[HW:HW + N_LAT * CY]
    left = jnp.pad(summed[..., :2 * HW], ((0, 0), (0, 0), (0, CX - 2 * HW))).reshape(N_LAT * CY, N_LON * CX)
    right = summed[..., 2 * HW:].reshape(N_LAT * CY, N_LON * CX)
    columns = jnp.pad(right, ((0, 0), (2 * HW, 0))) + jnp.pad(left, ((0, 0), (0, 2 * HW)))
    core = columns[:, HW:HW + N_LON * CX]
    wrapped_left = jnp.pad(columns[:, :HW], ((0, 0), (N_LON * CX - HW, 0)))
    wrapped_right = jnp.pad(columns[:, -HW:], ((0, 0), (0, N_LON * CX - HW)))
    return core + wrapped_left + wrapped_right


def reference(land_sea, obs_cell, obs_value, obs_weight, intersection, factors, coarse_inverse):
    ocean = land_sea.astype(jnp.float32)

    def cell_sums(cells, values):
        return jax.ops.segment_sum(values, cells, num_segments=CY * CX)

    obs_diag = tile_grid(jax.vmap(jax.vmap(cell_sums))(obs_cell, obs_weight))
    obs_load = tile_grid(jax.vmap(jax.vmap(cell_sums))(obs_cell, obs_weight * obs_value))
    rhs = ocean * obs_load

    ocean_pad = wrap_pad(ocean, 1)
    conduct = (ocean * ocean_pad[1:-1, 2:], ocean * ocean_pad[1:-1, :-2],
               ocean * ocean_pad[:-2, 1:-1], ocean * ocean_pad[2:, 1:-1])

    row_pos = jnp.arange(LAT_EXT, dtype=jnp.int32)
    col_pos = jnp.arange(LON_EXT, dtype=jnp.int32)
    reach = intersection.astype(jnp.int32)
    row_ok = (row_pos[None, :, None] >= HW - reach[:, None, :]) & (row_pos[None, :, None] < HW + CY + reach[:, None, :])
    col_ok = (col_pos[None, None, :] >= HW - reach[:, :, None]) & (col_pos[None, None, :] < HW + CX + reach[:, :, None])
    weights = to_tiles(ocean) * row_ok[..., None].astype(jnp.float32) * col_ok[:, None].astype(jnp.float32)
    blocks = factors.reshape(N_LAT, NBLK, BS, BS, N_LON * LON_EXT)

    def one_band(pair):
        band_factor, band_source = pair
        forward = jnp.einsum('kabx,kbx->kax', band_factor, band_source, precision=lax.Precision.HIGHEST)
        return jnp.einsum('kabx,kax->kbx', band_factor, forward, precision=lax.Precision.HIGHEST)

    def precondition(resid):
        source = (weights * to_tiles(resid)).reshape(N_LAT, NBLK, BS, N_LON * LON_EXT)
        solved = lax.map(one_band, (blocks, source))
        local = from_tiles(weights * solved.reshape(N_LAT, LAT_EXT, N_LON, LON_EXT))
        masked = (ocean * resid).reshape(N_LAT, SUB, CY // SUB, N_LON, SUB, CX // SUB)
        sums = jnp.sum(masked, axis=(2, 5))
        ordered = jnp.transpose(sums, (2, 0, 1, 3)).reshape(COARSE_ALL)
        answer = jnp.dot(coarse_inverse, ordered, precision=lax.Precision.HIGHEST, preferred_element_type=jnp.float32)
        placed = jnp.transpose(answer.reshape(N_LON, N_LAT, SUB, SUB), (1, 2, 0, 3))
        spread = jnp.broadcast_to(placed[:, :, None, :, :, None], (N_LAT, SUB, CY // SUB, N_LON, SUB, CX // SUB))
        return local + ocean * spread.reshape(N_LAT * CY, N_LON * CX)

    solution = jnp.zeros_like(rhs)
    residual = rhs
    precond = precondition(residual)
    first = precond
    affinity = jnp.sum(residual * precond)
    direction = precond
    for step in range(ITERS):
        image = operate(direction, ocean, obs_diag, conduct)
        alpha = affinity / jnp.sum(direction * image)
        solution = solution + alpha * direction
        residual = residual - alpha * image
        if step + 1 < ITERS:
            precond = precondition(residual)
            renewed = jnp.sum(residual * precond)
            direction = precond + (renewed / affinity) * direction
            affinity = renewed
    return solution, residual, first
```

```python
import functools

import jax
import jax.numpy as jnp
from jax import lax
from jax.experimental import pallas as pl
from jax.experimental.pallas import tpu as pltpu
from jax.sharding import PartitionSpec as P

HW = 16
SUB = 4
DAMPING = 0.02
LANES = 128
F32 = jnp.float32
BF16 = jnp.bfloat16


def iota(shape, dim):
    return lax.broadcasted_iota(jnp.int32, shape, dim)


def kernel(
    n_lat, n_lon,
    sea_ref, cell_ref, value_ref, weight_ref, reach_ref, factors_ref, coarse_ref,
    sol_ref, res_ref, pre_ref,
    fac, diag, core, wide, edge, edge_in, rows_in, corner_in, gather,
    contrib, side_in, band_in, cross_in, total, mine, lat_in, half, lon_in,
    fac_sem, send_sem, recv_sem,
):
    cy, cx = sea_ref.shape
    h, w = cy + 2 * HW, cx + 2 * HW
    i, j = lax.axis_index("lat"), lax.axis_index("lon")

    def lat_peer(o):
        return lax.rem(i + o + n_lat, n_lat)

    def lon_peer(o):
        return lax.rem(j + o + n_lon, n_lon)

    load = pltpu.make_async_copy(factors_ref, fac, fac_sem)
    load.start()

    barrier = pltpu.get_barrier_semaphore()

    def greet(pi, pj):
        pl.semaphore_signal(
            barrier, inc=1, device_id={"lat": pi, "lon": pj}, device_id_type=pl.DeviceIdType.MESH
        )

    corners = [(-1, -1), (-1, 1), (1, -1), (1, 1)]
    for o in range(1, n_lat):
        greet(lat_peer(o), j)
    for o in range(1, n_lon):
        greet(i, lon_peer(o))
    for di, dj in corners:
        greet(lat_peer(di), lon_peer(dj))

    used = [0]

    def remote(src, dst, pi, pj):
        k = used[0]
        used[0] += 1
        copy = pltpu.make_async_remote_copy(
            src_ref=src,
            dst_ref=dst,
            send_sem=send_sem.at[k],
            recv_sem=recv_sem.at[k],
            device_id={"lat": pi, "lon": pj},
            device_id_type=pl.DeviceIdType.MESH,
        )
        copy.start()
        return copy

    core[0, :, 0:cx] = sea_ref[...].astype(F32)
    core[0, :, cx:w] = jnp.zeros((cy, w - cx), F32)
    ocean = pltpu.roll(core[0], HW, 1)
    count = cell_ref.shape[1]
    chunk = 512 if count % 512 == 0 else count
    sums = jnp.zeros((4 * cy, w), F32)
    for at in range(0, count, chunk):
        cell = cell_ref[:, at : at + chunk].astype(F32)
        row = jnp.floor((cell + 0.5) * (1.0 / cx))
        col = cell - row * cx + HW
        weight = weight_ref[:, at : at + chunk]
        product = weight * value_ref[:, at : at + chunk]
        in_row = iota((cy, chunk), 0).astype(F32) == row
        in_col = iota((w, chunk), 0).astype(F32) == col
        parts = []
        for x in (weight, product):
            high = x.astype(BF16).astype(F32)
            parts += [high, x - high]
        left = jnp.concatenate([jnp.where(in_row, x, 0.0).astype(BF16) for x in parts], axis=0)
        right = jnp.where(in_col, 1.0, 0.0).astype(BF16)
        sums = sums + lax.dot_general(
            left, right, (((1,), (1,)), ((), ())), preferred_element_type=F32
        )
    diag[...] = sums[0:cy] + sums[cy : 2 * cy]
    rhs = ocean * (sums[2 * cy : 3 * cy] + sums[3 * cy : 4 * cy])
    core[0] = ocean
    core[1] = rhs

    block = cy // SUB
    lane_w = iota((SUB, w), 1) - HW
    sub_w = iota((SUB, w), 0) * (cx // SUB)
    group = jnp.where((lane_w >= sub_w) & (lane_w < sub_w + cx // SUB), 1.0, 0.0)
    strips = [
        jnp.sum(rhs[s * block : (s + 1) * block], axis=0, keepdims=True) * group for s in range(SUB)
    ]
    own = jnp.sum(jnp.concatenate(strips, axis=0), axis=1, keepdims=True)
    entries = SUB * SUB
    spot = iota((entries, LANES), 0) == (iota((entries, LANES), 1) % entries)
    own = jnp.sum(jnp.where(spot, own, 0.0), axis=0, keepdims=True)
    gather[j, i] = jnp.broadcast_to(own, (8, LANES))

    lane = iota((cy, LANES), 1)
    hi = w - LANES
    edge[0] = jnp.where(
        lane >= LANES - HW,
        pltpu.roll(ocean[:, :LANES], LANES - 2 * HW, 1),
        pltpu.roll(rhs[:, :LANES], LANES - 3 * HW, 1),
    )
    edge[1] = jnp.where(
        lane < HW, pltpu.roll(ocean[:, hi:], 2 * HW, 1), pltpu.roll(rhs[:, hi:], 3 * HW, 1)
    )

    pl.semaphore_wait(barrier, n_lat - 1 + n_lon - 1 + 4)

    first = [remote(gather.at[j, i], gather.at[j, i], lat_peer(o), j) for o in range(1, n_lat)]
    halo = [
        remote(edge.at[0], edge_in.at[1], i, lon_peer(-1)),
        remote(edge.at[1], edge_in.at[0], i, lon_peer(1)),
        remote(core.at[:, pl.ds(0, HW)], rows_in.at[1], lat_peer(-1), j),
        remote(core.at[:, pl.ds(cy - HW, HW)], rows_in.at[0], lat_peer(1), j),
    ]
    for k, (di, dj) in enumerate(corners):
        top = 0 if di < 0 else cy - HW
        halo.append(
            remote(
                edge.at[0 if dj < 0 else 1, pl.ds(top, HW)],
                corner_in.at[3 - k],
                lat_peer(di),
                lon_peer(dj),
            )
        )
    for copy in first:
        copy.wait_recv()
    for copy in first:
        copy.wait_send()
    second = [remote(gather.at[j], gather.at[j], i, lon_peer(o)) for o in range(1, n_lon)]
    for copy in halo:
        copy.wait()

    def west(x):
        at = iota(x.shape, 1)
        return (
            jnp.where(at < HW, x, 0.0),
            jnp.where(at < HW, pltpu.roll(x, LANES - HW, 1), 0.0),
        )

    def east(x):
        at = iota(x.shape, 1)
        return (
            jnp.where(at >= LANES - HW, x, 0.0),
            jnp.where(at >= LANES - HW, pltpu.roll(x, HW, 1), 0.0),
        )

    spans = (
        (0, HW, rows_in.at[0], corner_in[0], corner_in[1], jnp.where(i > 0, 1.0, 0.0)),
        (HW, cy, core, edge_in[0], edge_in[1], None),
        (HW + cy, HW, rows_in.at[1], corner_in[2], corner_in[3], jnp.where(i < n_lat - 1, 1.0, 0.0)),
    )
    for at, size, middle, left, right, inside in spans:
        for f, (lo, up) in enumerate(zip(west(left), east(right))):
            whole = middle[f]
            if inside is not None:
                whole, lo, up = whole * inside, lo * inside, up * inside
            wide[f, at : at + size, :] = whole
            wide[f, at : at + size, 0:LANES] += lo
            wide[f, at : at + size, hi:w] += up

    reach = reach_ref[0, 0]
    load.wait()
    col_pos = iota((HW, w), 1)
    col_ok = (col_pos >= HW - reach) & (col_pos < HW + cx + reach)
    blocks, size = fac.shape[0], fac.shape[1]
    for k in range(blocks):
        at = k * size
        row_pos = iota((size, w), 0) + at
        ok = col_ok & (row_pos >= HW - reach) & (row_pos < HW + cy + reach)
        scale = jnp.where(ok, wide[0, at : at + size], 0.0)
        u = scale * wide[1, at : at + size]
        g = jnp.zeros((size, w), F32)
        for p in range(size):
            row = fac[k, p]
            g = g + row * jnp.sum(row * u, axis=0, keepdims=True)
        contrib[at : at + size, :] = scale * g

    for copy in second:
        copy.wait()
    tiles = n_lat * n_lon
    per = LANES // entries
    ring = [
        jnp.where(iota((8, LANES), 1) // entries == r, 1.0, 0.0) for r in range(per)
    ]
    answer = jnp.zeros((entries, LANES), F32)
    for k in range(tiles // per):
        piece = jnp.zeros((8, LANES), F32)
        for r in range(per):
            d = k * per + r
            piece = piece + gather[d // n_lat, d % n_lat] * ring[r]
        answer = answer + coarse_ref[:, k * LANES : (k + 1) * LANES] * jnp.concatenate(
            [piece] * (entries // 8), axis=0
        )
    answer = jnp.sum(answer, axis=1, keepdims=True)
    for s in range(SUB):
        line = jnp.sum(answer[s * SUB : (s + 1) * SUB] * group, axis=0, keepdims=True)
        at = HW + s * block
        contrib[at : at + block, :] += core[0, s * block : (s + 1) * block, :] * line

    deep = 2 * HW
    back = [
        remote(contrib.at[:, pl.ds(0, LANES)], side_in.at[1], i, lon_peer(-1)),
        remote(contrib.at[:, pl.ds(hi, LANES)], side_in.at[0], i, lon_peer(1)),
        remote(contrib.at[pl.ds(0, deep)], band_in.at[1], lat_peer(-1), j),
        remote(contrib.at[pl.ds(h - deep, deep)], band_in.at[0], lat_peer(1), j),
    ]
    for k, (di, dj) in enumerate(corners):
        top = 0 if di < 0 else h - deep
        begin = 0 if dj < 0 else hi
        back.append(
            remote(
                contrib.at[pl.ds(top, deep), pl.ds(begin, LANES)],
                cross_in.at[3 - k],
                lat_peer(di),
                lon_peer(dj),
            )
        )
    total[...] = contrib[...]
    for copy in back:
        copy.wait()

    def from_west(x):
        return jnp.where(iota(x.shape, 1) < deep, pltpu.roll(x, deep, 1), 0.0)

    def from_east(x):
        return jnp.where(iota(x.shape, 1) >= LANES - deep, pltpu.roll(x, LANES - deep, 1), 0.0)

    total[:, 0:LANES] += from_west(side_in[0])
    total[:, hi:w] += from_east(side_in[1])
    for v in range(2):
        at = v * (h - deep)
        total[at : at + deep, :] += band_in[v]
        total[at : at + deep, 0:LANES] += from_west(cross_in[2 * v])
        total[at : at + deep, hi:w] += from_east(cross_in[2 * v + 1])

    p = total[HW : HW + cy, :]
    o = core[0]
    on, os = wide[0, HW - 1 : HW - 1 + cy, :], wide[0, HW + 1 : HW + 1 + cy, :]
    mid = wide[0, HW : HW + cy, :]
    oe, ow = pltpu.roll(mid, w - 1, 1), pltpu.roll(mid, 1, 1)
    beside = (
        oe * pltpu.roll(p, w - 1, 1)
        + ow * pltpu.roll(p, 1, 1)
        + on * total[HW - 1 : HW - 1 + cy, :]
        + os * total[HW + 1 : HW + 1 + cy, :]
    )
    image = o * ((diag[...] + DAMPING) * p + ((oe + ow + on + os) * p - beside)) + (1.0 - o) * p
    at = iota((cy, w), 1)
    inner = (at >= HW) & (at < HW + cx)

    def fold(x):
        x = jnp.sum(x.reshape(cy // 8, 8, w), axis=0)
        return sum(x[:, b : b + LANES] for b in range(0, w, LANES))

    mine[0] = fold(core[1] * p)
    mine[1] = fold(jnp.where(inner, p * image, 0.0))
    third = [remote(mine, lat_in.at[o - 1], lat_peer(o), j) for o in range(1, n_lat)]
    pre_ref[...] = pltpu.roll(p, w - HW, 1)[:, 0:cx]
    partial = mine[...]
    for o in range(1, n_lat):
        third[o - 1].wait()
        partial = partial + lat_in[o - 1]
    half[...] = partial
    fourth = [remote(half, lon_in.at[o - 1], i, lon_peer(o)) for o in range(1, n_lon)]
    rhs_out = pltpu.roll(core[1], w - HW, 1)[:, 0:cx]
    image_out = pltpu.roll(image, w - HW, 1)[:, 0:cx]
    for o in range(1, n_lon):
        fourth[o - 1].wait()
        partial = partial + lon_in[o - 1]
    rho = jnp.sum(partial[0], axis=(0, 1), keepdims=True)
    curve = jnp.sum(partial[1], axis=(0, 1), keepdims=True)
    alpha = rho / curve
    sol_ref[...] = alpha * pre_ref[...]
    res_ref[...] = rhs_out - alpha * image_out


def body(land_sea, obs_cell, obs_value, obs_weight, intersection, factors, coarse_inverse):
    n_lat, n_lon = lax.axis_size("lat"), lax.axis_size("lon")
    cy, cx = land_sea.shape
    h, w = cy + 2 * HW, cx + 2 * HW
    count = obs_cell.shape[-1]
    copies = 2 * (n_lat - 1 + n_lon - 1) + 16
    vmem = pl.BlockSpec(memory_space=pltpu.VMEM)
    out = jax.ShapeDtypeStruct((cy, cx), F32)
    return pl.pallas_call(
        functools.partial(kernel, n_lat, n_lon),
        out_shape=(out, out, out),
        in_specs=[
            vmem, vmem, vmem, vmem,
            pl.BlockSpec(memory_space=pltpu.SMEM),
            pl.BlockSpec(memory_space=pl.ANY),
            vmem,
        ],
        out_specs=(vmem, vmem, vmem),
        scratch_shapes=[
            pltpu.VMEM(factors.shape, F32),
            pltpu.VMEM((cy, w), F32),
            pltpu.VMEM((2, cy, w), F32),
            pltpu.VMEM((2, h, w), F32),
            pltpu.VMEM((2, cy, LANES), F32),
            pltpu.VMEM((2, cy, LANES), F32),
            pltpu.VMEM((2, 2, HW, w), F32),
            pltpu.VMEM((4, HW, LANES), F32),
            pltpu.VMEM((n_lon, n_lat, 8, LANES), F32),
            pltpu.VMEM((h, w), F32),
            pltpu.VMEM((2, h, LANES), F32),
            pltpu.VMEM((2, 2 * HW, w), F32),
            pltpu.VMEM((4, 2 * HW, LANES), F32),
            pltpu.VMEM((h, w), F32),
            pltpu.VMEM((2, 8, LANES), F32),
            pltpu.VMEM((n_lat - 1, 2, 8, LANES), F32),
            pltpu.VMEM((2, 8, LANES), F32),
            pltpu.VMEM((n_lon - 1, 2, 8, LANES), F32),
            pltpu.SemaphoreType.DMA,
            pltpu.SemaphoreType.DMA((copies,)),
            pltpu.SemaphoreType.DMA((copies,)),
        ],
        compiler_params=pltpu.CompilerParams(
            collective_id=0, has_side_effects=True, vmem_limit_bytes=40 * 1024 * 1024
        ),
    )(
        land_sea,
        obs_cell.reshape(1, count),
        obs_value.reshape(1, count),
        obs_weight.reshape(1, count),
        intersection,
        factors,
        coarse_inverse,
    )


def solution(mesh):
    in_specs = (
        P("lat", "lon"),
        P("lat", "lon", None),
        P("lat", "lon", None),
        P("lat", "lon", None),
        P("lat", "lon"),
        P("lat", None, None, "lon"),
        P(("lon", "lat"), None),
    )
    out_specs = (P("lat", "lon"), P("lat", "lon"), P("lat", "lon"))
    return jax.shard_map(body, mesh=mesh, in_specs=in_specs, out_specs=out_specs, check_vma=False)
```

```python
import functools

import jax
import jax.numpy as jnp
from jax import lax
from jax.experimental import pallas as pl
from jax.experimental.pallas import tpu as pltpu
from jax.sharding import PartitionSpec as P

HW = 16
SUB = 4
DAMPING = 0.02
LANES = 128
F32 = jnp.float32
BF16 = jnp.bfloat16


def iota(shape, dim):
    return lax.broadcasted_iota(jnp.int32, shape, dim)


QUARTER = 2 * HW


def pack(x, start):
    groups = LANES // QUARTER
    size = x.shape[0] // groups
    at = iota((size, LANES), 1) // QUARTER
    whole = jnp.zeros((size, LANES), F32)
    for g in range(groups):
        part = x[g * size : (g + 1) * size]
        shift = (g * QUARTER - start) % LANES
        part = pltpu.roll(part, shift, 1) if shift else part
        whole = jnp.where(at == g, part, whole)
    return whole


def unpack(x, start):
    groups = LANES // QUARTER
    at = iota(x.shape, 1)
    parts = []
    for g in range(groups):
        shift = (start - g * QUARTER) % LANES
        part = pltpu.roll(x, shift, 1) if shift else x
        parts.append(jnp.where((at >= start) & (at < start + QUARTER), part, 0.0))
    return jnp.concatenate(parts, axis=0)


def kernel(
    n_lat, n_lon,
    sea_hbm, cell_hbm, value_hbm, weight_hbm, reach_ref, factors_hbm, coarse_hbm,
    sol_ref, res_ref, pre_ref,
    sea_ref, cell_ref, value_ref, weight_ref, fac, coarse_ref,
    diag, core, wide, edge, edge_in, corner, rows_in, corner_in, near, gather,
    contrib, side, side_in, band_in, cross, cross_in, total, mine, lat_in, half, lon_in,
    load_sem, send_sem, recv_sem,
):
    cx, cy = sea_ref.shape
    h, w = cy + 2 * HW, cx + 2 * HW
    i, j = lax.axis_index("lat"), lax.axis_index("lon")

    def lat_peer(o):
        return lax.rem(i + o + n_lat, n_lat)

    def lon_peer(o):
        return lax.rem(j + o + n_lon, n_lon)

    loads = [
        pltpu.make_async_copy(src, dst, load_sem.at[k])
        for k, (src, dst) in enumerate(
            (
                (cell_hbm, cell_ref),
                (weight_hbm, weight_ref),
                (value_hbm, value_ref),
                (sea_hbm, sea_ref),
                (coarse_hbm, coarse_ref),
                (factors_hbm, fac),
            )
        )
    ]
    for load in loads:
        load.start()

    barrier = pltpu.get_barrier_semaphore()

    def greet(pi, pj):
        pl.semaphore_signal(
            barrier, inc=1, device_id={"lat": pi, "lon": pj}, device_id_type=pl.DeviceIdType.MESH
        )

    corners = [(-1, -1), (-1, 1), (1, -1), (1, 1)]
    for o in range(1, n_lat):
        greet(lat_peer(o), j)
    for o in range(1, n_lon):
        greet(i, lon_peer(o))
    for di, dj in corners:
        greet(lat_peer(di), lon_peer(dj))

    used = [0]

    def remote(src, dst, pi, pj):
        k = used[0]
        used[0] += 1
        copy = pltpu.make_async_remote_copy(
            src_ref=src,
            dst_ref=dst,
            send_sem=send_sem.at[k],
            recv_sem=recv_sem.at[k],
            device_id={"lat": pi, "lon": pj},
            device_id_type=pl.DeviceIdType.MESH,
        )
        copy.start()
        return copy

    for load in loads[:4]:
        load.wait()
    blank = jnp.zeros((HW, cy), F32)
    ocean = jnp.concatenate([blank, sea_ref[...].astype(F32), blank], axis=0).T
    count = cell_ref.shape[2]
    chunk = 512 if count % 512 == 0 else count
    sums = jnp.zeros((4 * cy, w), F32)
    for at in range(0, count, chunk):
        cell = cell_ref[0, :, at : at + chunk].astype(F32)
        row = jnp.floor((cell + 0.5) * (1.0 / cx))
        col = cell - row * cx + HW
        weight = weight_ref[0, :, at : at + chunk]
        product = weight * value_ref[0, :, at : at + chunk]
        in_row = iota((cy, chunk), 0).astype(F32) == row
        in_col = iota((w, chunk), 0).astype(F32) == col
        parts = []
        for x in (weight, product):
            high = x.astype(BF16).astype(F32)
            parts += [high, x - high]
        left = jnp.concatenate([jnp.where(in_row, x, 0.0).astype(BF16) for x in parts], axis=0)
        right = jnp.where(in_col, 1.0, 0.0).astype(BF16)
        sums = sums + lax.dot_general(
            left, right, (((1,), (1,)), ((), ())), preferred_element_type=F32
        )
    diag[...] = sums[0:cy] + sums[cy : 2 * cy]
    rhs = ocean * (sums[2 * cy : 3 * cy] + sums[3 * cy : 4 * cy])
    core[0] = ocean
    core[1] = rhs

    block = cy // SUB
    lane_w = iota((SUB, w), 1) - HW
    sub_w = iota((SUB, w), 0) * (cx // SUB)
    group = jnp.where((lane_w >= sub_w) & (lane_w < sub_w + cx // SUB), 1.0, 0.0)
    strips = [
        jnp.sum(rhs[s * block : (s + 1) * block], axis=0, keepdims=True) * group for s in range(SUB)
    ]
    own = jnp.sum(jnp.concatenate(strips, axis=0), axis=1, keepdims=True)
    entries = SUB * SUB
    spot = iota((entries, LANES), 0) == (iota((entries, LANES), 1) % entries)
    own = jnp.sum(jnp.where(spot, own, 0.0), axis=0, keepdims=True)
    near[i] = own

    lane = iota((cy, LANES), 1)
    hi = w - LANES
    left = jnp.where(lane < QUARTER, ocean[:, :LANES], pltpu.roll(rhs[:, :LANES], HW, 1))
    right = jnp.where(lane >= LANES - HW, pltpu.roll(rhs[:, hi:], HW, 1), ocean[:, hi:])
    strips = (left, HW), (right, LANES - 2 * HW)
    for v, (x, start) in enumerate(strips):
        edge[v] = pack(x, start)
    for k, (di, dj) in enumerate(corners):
        x = strips[0 if dj < 0 else 1][0]
        corner[k] = x[0:HW] if di < 0 else x[cy - HW : cy]

    pl.semaphore_wait(barrier, n_lat - 1 + n_lon - 1 + 4)

    first = [remote(near.at[i], near.at[i], lat_peer(o), j) for o in range(1, n_lat)]
    halo = [
        remote(edge.at[0], edge_in.at[1], i, lon_peer(-1)),
        remote(edge.at[1], edge_in.at[0], i, lon_peer(1)),
        remote(core.at[:, pl.ds(0, HW)], rows_in.at[1], lat_peer(-1), j),
        remote(core.at[:, pl.ds(cy - HW, HW)], rows_in.at[0], lat_peer(1), j),
    ]
    for k, (di, dj) in enumerate(corners):
        halo.append(remote(corner.at[k], corner_in.at[3 - k], lat_peer(di), lon_peer(dj)))
    for copy in first:
        copy.wait()
    per = LANES // entries
    slot = iota((1, LANES), 1) // entries
    joint = min(n_lat, per)
    for q in range(n_lat // joint):
        line = jnp.zeros((1, LANES), F32)
        for r in range(joint):
            line = jnp.where(slot % joint == r, near[q * joint + r], line)
        gather[j, q] = line
    second = [remote(gather.at[j], gather.at[j], i, lon_peer(o)) for o in range(1, n_lon)]
    for copy in halo:
        copy.wait()

    def west(x):
        at = iota(x.shape, 1)
        return (
            jnp.where(at < HW, pltpu.roll(x, 2 * HW, 1), 0.0),
            jnp.where(at < HW, pltpu.roll(x, HW, 1), 0.0),
        )

    def east(x):
        at = iota(x.shape, 1)
        return (
            jnp.where(at >= LANES - HW, pltpu.roll(x, LANES - 2 * HW, 1), 0.0),
            jnp.where(at >= LANES - HW, pltpu.roll(x, LANES - 3 * HW, 1), 0.0),
        )

    spans = (
        (0, HW, rows_in.at[0], corner_in[0], corner_in[1], jnp.where(i > 0, 1.0, 0.0)),
        (HW, cy, core, unpack(edge_in[0], LANES - QUARTER), unpack(edge_in[1], HW), None),
        (HW + cy, HW, rows_in.at[1], corner_in[2], corner_in[3], jnp.where(i < n_lat - 1, 1.0, 0.0)),
    )
    for at, size, middle, left, right, inside in spans:
        for f, (lo, up) in enumerate(zip(west(left), east(right))):
            whole = middle[f]
            if inside is not None:
                whole, lo, up = whole * inside, lo * inside, up * inside
            wide[f, at : at + size, :] = whole
            wide[f, at : at + size, 0:LANES] += lo
            wide[f, at : at + size, hi:w] += up

    reach = reach_ref[0, 0]
    for load in loads[4:]:
        load.wait()
    col_pos = iota((HW, w), 1)
    col_ok = (col_pos >= HW - reach) & (col_pos < HW + cx + reach)
    blocks, size = fac.shape[0], fac.shape[1]
    for k in range(blocks):
        at = k * size
        row_pos = iota((size, w), 0) + at
        ok = col_ok & (row_pos >= HW - reach) & (row_pos < HW + cy + reach)
        scale = jnp.where(ok, wide[0, at : at + size], 0.0)
        u = scale * wide[1, at : at + size]
        g = jnp.zeros((size, w), F32)
        for p in range(size):
            row = fac[k, p]
            g = g + row * jnp.sum(row * u, axis=0, keepdims=True)
        contrib[at : at + size, :] = scale * g

    for copy in second:
        copy.wait()
    answer = jnp.zeros((entries, LANES), F32)
    for k in range(n_lat * n_lon // per):
        piece = jnp.zeros((1, LANES), F32)
        for r in range(0, per, joint):
            d = k * per + r
            piece = jnp.where(slot // joint == r // joint, gather[d // n_lat, d % n_lat // joint], piece)
        answer = answer + coarse_ref[:, k * LANES : (k + 1) * LANES] * piece
    answer = jnp.sum(answer, axis=1, keepdims=True)
    for s in range(SUB):
        line = jnp.sum(answer[s * SUB : (s + 1) * SUB] * group, axis=0, keepdims=True)
        at = HW + s * block
        contrib[at : at + block, :] += core[0, s * block : (s + 1) * block, :] * line

    deep = 2 * HW
    side[0] = pack(contrib[:, 0:LANES], 0)
    side[1] = pack(contrib[:, hi:w], LANES - deep)
    for k, (di, dj) in enumerate(corners):
        top = 0 if di < 0 else h - deep
        begin, start = (0, 0) if dj < 0 else (hi, LANES - deep)
        cross[k] = pack(contrib[top : top + deep, begin : begin + LANES], start)
    back = [
        remote(side.at[0], side_in.at[1], i, lon_peer(-1)),
        remote(side.at[1], side_in.at[0], i, lon_peer(1)),
        remote(contrib.at[pl.ds(0, deep)], band_in.at[1], lat_peer(-1), j),
        remote(contrib.at[pl.ds(h - deep, deep)], band_in.at[0], lat_peer(1), j),
    ]
    for k, (di, dj) in enumerate(corners):
        back.append(remote(cross.at[k], cross_in.at[3 - k], lat_peer(di), lon_peer(dj)))
    total[...] = contrib[...]
    for copy in back:
        copy.wait()

    total[:, 0:LANES] += unpack(side_in[0], 0)
    total[:, hi:w] += unpack(side_in[1], LANES - deep)
    for v in range(2):
        at = v * (h - deep)
        total[at : at + deep, :] += band_in[v]
        total[at : at + deep, 0:LANES] += unpack(cross_in[2 * v], 0)
        total[at : at + deep, hi:w] += unpack(cross_in[2 * v + 1], LANES - deep)

    p = total[HW : HW + cy, :]
    o = core[0]
    on, os = wide[0, HW - 1 : HW - 1 + cy, :], wide[0, HW + 1 : HW + 1 + cy, :]
    mid = wide[0, HW : HW + cy, :]
    oe, ow = pltpu.roll(mid, w - 1, 1), pltpu.roll(mid, 1, 1)
    beside = (
        oe * pltpu.roll(p, w - 1, 1)
        + ow * pltpu.roll(p, 1, 1)
        + on * total[HW - 1 : HW - 1 + cy, :]
        + os * total[HW + 1 : HW + 1 + cy, :]
    )
    image = o * ((diag[...] + DAMPING) * p + ((oe + ow + on + os) * p - beside)) + (1.0 - o) * p
    at = iota((cy, w), 1)
    inner = (at >= HW) & (at < HW + cx)

    def fold(x):
        x = jnp.sum(x, axis=0, keepdims=True)
        return sum(x[:, b : b + LANES] for b in range(0, w, LANES))

    mine[0:1] = fold(core[1] * p)
    mine[1:2] = fold(jnp.where(inner, p * image, 0.0))
    third = [remote(mine, lat_in.at[o - 1], lat_peer(o), j) for o in range(1, n_lat)]
    pre_ref[...] = p.T[HW : HW + cx]
    partial = mine[...]
    for o in range(1, n_lat):
        third[o - 1].wait()
        partial = partial + lat_in[o - 1]
    half[...] = partial
    fourth = [remote(half, lon_in.at[o - 1], i, lon_peer(o)) for o in range(1, n_lon)]
    rhs_out = core[1].T[HW : HW + cx]
    image_out = image.T[HW : HW + cx]
    for o in range(1, n_lon):
        fourth[o - 1].wait()
        partial = partial + lon_in[o - 1]
    rho = jnp.sum(partial[0:1], axis=1, keepdims=True)
    curve = jnp.sum(partial[1:2], axis=1, keepdims=True)
    alpha = rho / curve
    sol_ref[...] = alpha * pre_ref[...]
    res_ref[...] = rhs_out - alpha * image_out


def body(land_sea, obs_cell, obs_value, obs_weight, intersection, factors, coarse_inverse):
    n_lat, n_lon = lax.axis_size("lat"), lax.axis_size("lon")
    cy, cx = land_sea.shape
    h, w = cy + 2 * HW, cx + 2 * HW
    copies = 2 * (n_lat - 1 + n_lon - 1) + 16
    vmem = pl.BlockSpec(memory_space=pltpu.VMEM)
    entries = SUB * SUB
    lines = n_lat // min(n_lat, LANES // entries)
    hbm = pl.BlockSpec(memory_space=pltpu.HBM)
    out = jax.ShapeDtypeStruct((cx, cy), F32)
    results = pl.pallas_call(
        functools.partial(kernel, n_lat, n_lon),
        out_shape=(out, out, out),
        in_specs=[hbm, hbm, hbm, hbm, pl.BlockSpec(memory_space=pltpu.SMEM), hbm, hbm],
        out_specs=(vmem, vmem, vmem),
        scratch_shapes=[
            pltpu.VMEM((cx, cy), jnp.int32),
            pltpu.VMEM(obs_cell.shape, jnp.int32),
            pltpu.VMEM(obs_value.shape, F32),
            pltpu.VMEM(obs_weight.shape, F32),
            pltpu.VMEM(factors.shape, F32),
            pltpu.VMEM(coarse_inverse.shape, F32),
            pltpu.VMEM((cy, w), F32),
            pltpu.VMEM((2, cy, w), F32),
            pltpu.VMEM((2, h, w), F32),
            pltpu.VMEM((2, cy // 4, LANES), F32),
            pltpu.VMEM((2, cy // 4, LANES), F32),
            pltpu.VMEM((4, HW, LANES), F32),
            pltpu.VMEM((2, 2, HW, w), F32),
            pltpu.VMEM((4, HW, LANES), F32),
            pltpu.VMEM((n_lat, 1, LANES), F32),
            pltpu.VMEM((n_lon, lines, 1, LANES), F32),
            pltpu.VMEM((h, w), F32),
            pltpu.VMEM((2, h // 4, LANES), F32),
            pltpu.VMEM((2, h // 4, LANES), F32),
            pltpu.VMEM((2, 2 * HW, w), F32),
            pltpu.VMEM((4, HW // 2, LANES), F32),
            pltpu.VMEM((4, HW // 2, LANES), F32),
            pltpu.VMEM((h, w), F32),
            pltpu.VMEM((2, LANES), F32),
            pltpu.VMEM((n_lat - 1, 2, LANES), F32),
            pltpu.VMEM((2, LANES), F32),
            pltpu.VMEM((n_lon - 1, 2, LANES), F32),
            pltpu.SemaphoreType.DMA((6,)),
            pltpu.SemaphoreType.DMA((copies,)),
            pltpu.SemaphoreType.DMA((copies,)),
        ],
        compiler_params=pltpu.CompilerParams(
            collective_id=0, has_side_effects=True, vmem_limit_bytes=64 * 1024 * 1024
        ),
    )(land_sea.T, obs_cell, obs_value, obs_weight, intersection, factors, coarse_inverse)
    return tuple(x.T for x in results)


def solution(mesh):
    in_specs = (
        P("lat", "lon"),
        P("lat", "lon", None),
        P("lat", "lon", None),
        P("lat", "lon", None),
        P("lat", "lon"),
        P("lat", None, None, "lon"),
        P(("lon", "lat"), None),
    )
    out_specs = (P("lat", "lon"), P("lat", "lon"), P("lat", "lon"))
    return jax.shard_map(body, mesh=mesh, in_specs=in_specs, out_specs=out_specs, check_vma=False)
```

```python
import functools

import jax
import jax.numpy as jnp
from jax import lax
from jax.experimental import pallas as pl
from jax.experimental.pallas import tpu as pltpu
from jax.sharding import PartitionSpec as P

HW = 16
SUB = 4
DAMPING = 0.02
LANES = 128
F32 = jnp.float32
BF16 = jnp.bfloat16


def iota(shape, dim):
    return lax.broadcasted_iota(jnp.int32, shape, dim)


QUARTER = 2 * HW


def pack(x, start):
    groups = LANES // QUARTER
    size = x.shape[0] // groups
    at = iota((size, LANES), 1) // QUARTER
    whole = jnp.zeros((size, LANES), F32)
    for g in range(groups):
        part = x[g * size : (g + 1) * size]
        shift = (g * QUARTER - start) % LANES
        part = pltpu.roll(part, shift, 1) if shift else part
        whole = jnp.where(at == g, part, whole)
    return whole


def unpack(x, start):
    groups = LANES // QUARTER
    at = iota(x.shape, 1)
    parts = []
    for g in range(groups):
        shift = (start - g * QUARTER) % LANES
        part = pltpu.roll(x, shift, 1) if shift else x
        parts.append(jnp.where((at >= start) & (at < start + QUARTER), part, 0.0))
    return jnp.concatenate(parts, axis=0)


def kernel(
    n_lat, n_lon,
    sea_hbm, cell_hbm, value_hbm, weight_hbm, reach_ref, factors_hbm, coarse_hbm,
    pre_hbm, rhs_hbm, image_hbm, alpha_ref,
    sea_ref, cell_ref, value_ref, weight_ref, fac, coarse_ref,
    diag, core, wide, edge, edge_in, corner, rows_in, corner_in, near, gather,
    contrib, side, side_in, band_in, cross, cross_in, total, mine, lat_in, half, lon_in, out,
    load_sem, store_sem, send_sem, recv_sem,
):
    cx, cy = sea_ref.shape
    h, w = cy + 2 * HW, cx + 2 * HW
    i, j = lax.axis_index("lat"), lax.axis_index("lon")

    def lat_peer(o):
        return lax.rem(i + o + n_lat, n_lat)

    def lon_peer(o):
        return lax.rem(j + o + n_lon, n_lon)

    loads = [
        pltpu.make_async_copy(src, dst, load_sem.at[k])
        for k, (src, dst) in enumerate(
            (
                (cell_hbm, cell_ref),
                (weight_hbm, weight_ref),
                (value_hbm, value_ref),
                (sea_hbm, sea_ref),
                (coarse_hbm, coarse_ref),
                (factors_hbm, fac),
            )
        )
    ]
    for load in loads:
        load.start()

    barrier = pltpu.get_barrier_semaphore()

    def greet(pi, pj):
        pl.semaphore_signal(
            barrier, inc=1, device_id={"lat": pi, "lon": pj}, device_id_type=pl.DeviceIdType.MESH
        )

    corners = [(-1, -1), (-1, 1), (1, -1), (1, 1)]
    for o in range(1, n_lat):
        greet(lat_peer(o), j)
    for o in range(1, n_lon):
        greet(i, lon_peer(o))
    for di, dj in corners:
        greet(lat_peer(di), lon_peer(dj))

    used = [0]

    def remote(src, dst, pi, pj):
        k = used[0]
        used[0] += 1
        copy = pltpu.make_async_remote_copy(
            src_ref=src,
            dst_ref=dst,
            send_sem=send_sem.at[k],
            recv_sem=recv_sem.at[k],
            device_id={"lat": pi, "lon": pj},
            device_id_type=pl.DeviceIdType.MESH,
        )
        copy.start()
        return copy

    for load in loads[:4]:
        load.wait()
    blank = jnp.zeros((HW, cy), F32)
    ocean = jnp.concatenate([blank, sea_ref[...].astype(F32), blank], axis=0).T
    count = cell_ref.shape[2]
    chunk = 512 if count % 512 == 0 else count
    sums = jnp.zeros((4 * cy, w), F32)
    for at in range(0, count, chunk):
        cell = cell_ref[0, :, at : at + chunk].astype(F32)
        row = jnp.floor((cell + 0.5) * (1.0 / cx))
        col = cell - row * cx + HW
        weight = weight_ref[0, :, at : at + chunk]
        product = weight * value_ref[0, :, at : at + chunk]
        in_row = iota((cy, chunk), 0).astype(F32) == row
        in_col = iota((w, chunk), 0).astype(F32) == col
        parts = []
        for x in (weight, product):
            high = x.astype(BF16).astype(F32)
            parts += [high, x - high]
        left = jnp.concatenate([jnp.where(in_row, x, 0.0).astype(BF16) for x in parts], axis=0)
        right = jnp.where(in_col, 1.0, 0.0).astype(BF16)
        sums = sums + lax.dot_general(
            left, right, (((1,), (1,)), ((), ())), preferred_element_type=F32
        )
    diag[...] = sums[0:cy] + sums[cy : 2 * cy]
    rhs = ocean * (sums[2 * cy : 3 * cy] + sums[3 * cy : 4 * cy])
    core[0] = ocean
    core[1] = rhs

    block = cy // SUB
    lane_w = iota((SUB, w), 1) - HW
    sub_w = iota((SUB, w), 0) * (cx // SUB)
    group = jnp.where((lane_w >= sub_w) & (lane_w < sub_w + cx // SUB), 1.0, 0.0)
    strips = [
        jnp.sum(rhs[s * block : (s + 1) * block], axis=0, keepdims=True) * group for s in range(SUB)
    ]
    own = jnp.sum(jnp.concatenate(strips, axis=0), axis=1, keepdims=True)
    entries = SUB * SUB
    spot = iota((entries, LANES), 0) == (iota((entries, LANES), 1) % entries)
    own = jnp.sum(jnp.where(spot, own, 0.0), axis=0, keepdims=True)
    near[i] = own

    lane = iota((cy, LANES), 1)
    hi = w - LANES
    left = jnp.where(lane < QUARTER, ocean[:, :LANES], pltpu.roll(rhs[:, :LANES], HW, 1))
    right = jnp.where(lane >= LANES - HW, pltpu.roll(rhs[:, hi:], HW, 1), ocean[:, hi:])
    strips = (left, HW), (right, LANES - 2 * HW)
    for v, (x, start) in enumerate(strips):
        edge[v] = pack(x, start)
    for k, (di, dj) in enumerate(corners):
        x = strips[0 if dj < 0 else 1][0]
        corner[k] = x[0:HW] if di < 0 else x[cy - HW : cy]

    pl.semaphore_wait(barrier, n_lat - 1 + n_lon - 1 + 4)

    first = [remote(near.at[i], near.at[i], lat_peer(o), j) for o in range(1, n_lat)]
    halo = [
        remote(edge.at[0], edge_in.at[1], i, lon_peer(-1)),
        remote(edge.at[1], edge_in.at[0], i, lon_peer(1)),
        remote(core.at[:, pl.ds(0, HW)], rows_in.at[1], lat_peer(-1), j),
        remote(core.at[:, pl.ds(cy - HW, HW)], rows_in.at[0], lat_peer(1), j),
    ]
    for k, (di, dj) in enumerate(corners):
        halo.append(remote(corner.at[k], corner_in.at[3 - k], lat_peer(di), lon_peer(dj)))
    for copy in first:
        copy.wait()
    per = LANES // entries
    slot = iota((1, LANES), 1) // entries
    joint = min(n_lat, per)
    for q in range(n_lat // joint):
        line = jnp.zeros((1, LANES), F32)
        for r in range(joint):
            line = jnp.where(slot % joint == r, near[q * joint + r], line)
        gather[j, q] = line
    second = [remote(gather.at[j], gather.at[j], i, lon_peer(o)) for o in range(1, n_lon)]
    for copy in halo:
        copy.wait()

    def west(x):
        at = iota(x.shape, 1)
        return (
            jnp.where(at < HW, pltpu.roll(x, 2 * HW, 1), 0.0),
            jnp.where(at < HW, pltpu.roll(x, HW, 1), 0.0),
        )

    def east(x):
        at = iota(x.shape, 1)
        return (
            jnp.where(at >= LANES - HW, pltpu.roll(x, LANES - 2 * HW, 1), 0.0),
            jnp.where(at >= LANES - HW, pltpu.roll(x, LANES - 3 * HW, 1), 0.0),
        )

    spans = (
        (0, HW, rows_in.at[0], corner_in[0], corner_in[1], jnp.where(i > 0, 1.0, 0.0)),
        (HW, cy, core, unpack(edge_in[0], LANES - QUARTER), unpack(edge_in[1], HW), None),
        (HW + cy, HW, rows_in.at[1], corner_in[2], corner_in[3], jnp.where(i < n_lat - 1, 1.0, 0.0)),
    )
    for at, size, middle, left, right, inside in spans:
        for f, (lo, up) in enumerate(zip(west(left), east(right))):
            whole = middle[f]
            if inside is not None:
                whole, lo, up = whole * inside, lo * inside, up * inside
            wide[f, at : at + size, :] = whole
            wide[f, at : at + size, 0:LANES] += lo
            wide[f, at : at + size, hi:w] += up

    reach = reach_ref[0, 0]
    for load in loads[4:]:
        load.wait()
    col_pos = iota((HW, w), 1)
    col_ok = (col_pos >= HW - reach) & (col_pos < HW + cx + reach)
    blocks, size = fac.shape[0], fac.shape[1]
    for k in range(blocks):
        at = k * size
        row_pos = iota((size, w), 0) + at
        ok = col_ok & (row_pos >= HW - reach) & (row_pos < HW + cy + reach)
        scale = jnp.where(ok, wide[0, at : at + size], 0.0)
        u = scale * wide[1, at : at + size]
        g = jnp.zeros((size, w), F32)
        for p in range(size):
            row = fac[k, p]
            g = g + row * jnp.sum(row * u, axis=0, keepdims=True)
        contrib[at : at + size, :] = scale * g

    for copy in second:
        copy.wait()
    answer = jnp.zeros((entries, LANES), F32)
    for k in range(n_lat * n_lon // per):
        piece = jnp.zeros((1, LANES), F32)
        for r in range(0, per, joint):
            d = k * per + r
            piece = jnp.where(slot // joint == r // joint, gather[d // n_lat, d % n_lat // joint], piece)
        answer = answer + coarse_ref[:, k * LANES : (k + 1) * LANES] * piece
    answer = jnp.sum(answer, axis=1, keepdims=True)
    for s in range(SUB):
        line = jnp.sum(answer[s * SUB : (s + 1) * SUB] * group, axis=0, keepdims=True)
        at = HW + s * block
        contrib[at : at + block, :] += core[0, s * block : (s + 1) * block, :] * line

    deep = 2 * HW
    side[0] = pack(contrib[:, 0:LANES], 0)
    side[1] = pack(contrib[:, hi:w], LANES - deep)
    for k, (di, dj) in enumerate(corners):
        top = 0 if di < 0 else h - deep
        begin, start = (0, 0) if dj < 0 else (hi, LANES - deep)
        cross[k] = pack(contrib[top : top + deep, begin : begin + LANES], start)
    back = [
        remote(side.at[0], side_in.at[1], i, lon_peer(-1)),
        remote(side.at[1], side_in.at[0], i, lon_peer(1)),
        remote(contrib.at[pl.ds(0, deep)], band_in.at[1], lat_peer(-1), j),
        remote(contrib.at[pl.ds(h - deep, deep)], band_in.at[0], lat_peer(1), j),
    ]
    for k, (di, dj) in enumerate(corners):
        back.append(remote(cross.at[k], cross_in.at[3 - k], lat_peer(di), lon_peer(dj)))
    total[...] = contrib[...]
    for copy in back:
        copy.wait()

    total[:, 0:LANES] += unpack(side_in[0], 0)
    total[:, hi:w] += unpack(side_in[1], LANES - deep)
    for v in range(2):
        at = v * (h - deep)
        total[at : at + deep, :] += band_in[v]
        total[at : at + deep, 0:LANES] += unpack(cross_in[2 * v], 0)
        total[at : at + deep, hi:w] += unpack(cross_in[2 * v + 1], LANES - deep)

    p = total[HW : HW + cy, :]
    o = core[0]
    on, os = wide[0, HW - 1 : HW - 1 + cy, :], wide[0, HW + 1 : HW + 1 + cy, :]
    mid = wide[0, HW : HW + cy, :]
    oe, ow = pltpu.roll(mid, w - 1, 1), pltpu.roll(mid, 1, 1)
    beside = (
        oe * pltpu.roll(p, w - 1, 1)
        + ow * pltpu.roll(p, 1, 1)
        + on * total[HW - 1 : HW - 1 + cy, :]
        + os * total[HW + 1 : HW + 1 + cy, :]
    )
    image = o * ((diag[...] + DAMPING) * p + ((oe + ow + on + os) * p - beside)) + (1.0 - o) * p
    at = iota((cy, w), 1)
    inner = (at >= HW) & (at < HW + cx)

    def fold(x):
        x = jnp.sum(x, axis=0, keepdims=True)
        return sum(x[:, b : b + LANES] for b in range(0, w, LANES))

    mine[0:1] = fold(core[1] * p)
    mine[1:2] = fold(jnp.where(inner, p * image, 0.0))
    third = [remote(mine, lat_in.at[o - 1], lat_peer(o), j) for o in range(1, n_lat)]
    stores = []
    for k, (x, dst) in enumerate(((p, pre_hbm), (core[1], rhs_hbm), (image, image_hbm))):
        out[k] = x.T[HW : HW + cx]
        stores.append(pltpu.make_async_copy(out.at[k], dst, store_sem.at[k]))
        stores[k].start()
    partial = mine[...]
    for o in range(1, n_lat):
        third[o - 1].wait()
        partial = partial + lat_in[o - 1]
    half[...] = partial
    fourth = [remote(half, lon_in.at[o - 1], i, lon_peer(o)) for o in range(1, n_lon)]
    for o in range(1, n_lon):
        fourth[o - 1].wait()
        partial = partial + lon_in[o - 1]
    rho = jnp.sum(partial[0:1], axis=1, keepdims=True)
    curve = jnp.sum(partial[1:2], axis=1, keepdims=True)
    alpha_ref[...] = jnp.broadcast_to(rho / curve, alpha_ref.shape)
    for store in stores:
        store.wait()


def finish(pre_ref, rhs_ref, image_ref, alpha_ref, sol_ref, res_ref, out_ref):
    alpha = alpha_ref[0:1, 0:1]
    pre = pre_ref[...]
    out_ref[...] = pre
    sol_ref[...] = alpha * pre
    res_ref[...] = rhs_ref[...] - alpha * image_ref[...]


def body(land_sea, obs_cell, obs_value, obs_weight, intersection, factors, coarse_inverse):
    n_lat, n_lon = lax.axis_size("lat"), lax.axis_size("lon")
    cy, cx = land_sea.shape
    h, w = cy + 2 * HW, cx + 2 * HW
    copies = 2 * (n_lat - 1 + n_lon - 1) + 16
    vmem = pl.BlockSpec(memory_space=pltpu.VMEM)
    entries = SUB * SUB
    lines = n_lat // min(n_lat, LANES // entries)
    hbm = pl.BlockSpec(memory_space=pltpu.HBM)
    out = jax.ShapeDtypeStruct((cx, cy), F32)
    fields = pl.pallas_call(
        functools.partial(kernel, n_lat, n_lon),
        out_shape=(out, out, out, jax.ShapeDtypeStruct((8, LANES), F32)),
        in_specs=[hbm, hbm, hbm, hbm, pl.BlockSpec(memory_space=pltpu.SMEM), hbm, hbm],
        out_specs=(hbm, hbm, hbm, vmem),
        scratch_shapes=[
            pltpu.VMEM((cx, cy), jnp.int32),
            pltpu.VMEM(obs_cell.shape, jnp.int32),
            pltpu.VMEM(obs_value.shape, F32),
            pltpu.VMEM(obs_weight.shape, F32),
            pltpu.VMEM(factors.shape, F32),
            pltpu.VMEM(coarse_inverse.shape, F32),
            pltpu.VMEM((cy, w), F32),
            pltpu.VMEM((2, cy, w), F32),
            pltpu.VMEM((2, h, w), F32),
            pltpu.VMEM((2, cy // 4, LANES), F32),
            pltpu.VMEM((2, cy // 4, LANES), F32),
            pltpu.VMEM((4, HW, LANES), F32),
            pltpu.VMEM((2, 2, HW, w), F32),
            pltpu.VMEM((4, HW, LANES), F32),
            pltpu.VMEM((n_lat, 1, LANES), F32),
            pltpu.VMEM((n_lon, lines, 1, LANES), F32),
            pltpu.VMEM((h, w), F32),
            pltpu.VMEM((2, h // 4, LANES), F32),
            pltpu.VMEM((2, h // 4, LANES), F32),
            pltpu.VMEM((2, 2 * HW, w), F32),
            pltpu.VMEM((4, HW // 2, LANES), F32),
            pltpu.VMEM((4, HW // 2, LANES), F32),
            pltpu.VMEM((h, w), F32),
            pltpu.VMEM((2, LANES), F32),
            pltpu.VMEM((n_lat - 1, 2, LANES), F32),
            pltpu.VMEM((2, LANES), F32),
            pltpu.VMEM((n_lon - 1, 2, LANES), F32),
            pltpu.VMEM((3, cx, cy), F32),
            pltpu.SemaphoreType.DMA((6,)),
            pltpu.SemaphoreType.DMA((3,)),
            pltpu.SemaphoreType.DMA((copies,)),
            pltpu.SemaphoreType.DMA((copies,)),
        ],
        compiler_params=pltpu.CompilerParams(
            collective_id=0, has_side_effects=True, vmem_limit_bytes=64 * 1024 * 1024
        ),
    )(land_sea.T, obs_cell, obs_value, obs_weight, intersection, factors, coarse_inverse)
    results = pl.pallas_call(
        finish,
        out_shape=(out, out, out),
        in_specs=[vmem] * 4,
        out_specs=(vmem, vmem, vmem),
        compiler_params=pltpu.CompilerParams(vmem_limit_bytes=64 * 1024 * 1024),
    )(*fields)
    return tuple(x.T for x in results)


def solution(mesh):
    in_specs = (
        P("lat", "lon"),
        P("lat", "lon", None),
        P("lat", "lon", None),
        P("lat", "lon", None),
        P("lat", "lon"),
        P("lat", None, None, "lon"),
        P(("lon", "lat"), None),
    )
    out_specs = (P("lat", "lon"), P("lat", "lon"), P("lat", "lon"))
    return jax.shard_map(body, mesh=mesh, in_specs=in_specs, out_specs=out_specs, check_vma=False)
```

```python
import functools

import jax
import jax.numpy as jnp
from jax import lax
from jax.experimental import pallas as pl
from jax.experimental.pallas import tpu as pltpu
from jax.sharding import PartitionSpec as P

HW = 16
SUB = 4
DAMPING = 0.02
LANES = 128
F32 = jnp.float32
BF16 = jnp.bfloat16


def iota(shape, dim):
    return lax.broadcasted_iota(jnp.int32, shape, dim)


QUARTER = 2 * HW


def pack(x, start):
    groups = LANES // QUARTER
    size = x.shape[0] // groups
    at = iota((size, LANES), 1) // QUARTER
    whole = jnp.zeros((size, LANES), F32)
    for g in range(groups):
        part = x[g * size : (g + 1) * size]
        shift = (g * QUARTER - start) % LANES
        part = pltpu.roll(part, shift, 1) if shift else part
        whole = jnp.where(at == g, part, whole)
    return whole


def unpack(x, start):
    groups = LANES // QUARTER
    at = iota(x.shape, 1)
    parts = []
    for g in range(groups):
        shift = (start - g * QUARTER) % LANES
        part = pltpu.roll(x, shift, 1) if shift else x
        parts.append(jnp.where((at >= start) & (at < start + QUARTER), part, 0.0))
    return jnp.concatenate(parts, axis=0)


def kernel(
    n_lat, n_lon,
    sea_hbm, cell_hbm, value_hbm, weight_hbm, reach_ref, factors_hbm, coarse_hbm,
    pre_hbm, rhs_hbm, image_hbm, alpha_ref,
    sea_ref, cell_ref, value_ref, weight_ref, fac, coarse_ref,
    diag, core, wide, edge, edge_in, corner, rows_in, corner_in, near, gather,
    contrib, side, side_in, band_in, cross, cross_in, total, mine, lat_in, half, lon_in, out,
    load_sem, store_sem, send_sem, recv_sem,
):
    cx, cy = sea_ref.shape
    h, w = cy + 2 * HW, cx + 2 * HW
    i, j = lax.axis_index("lat"), lax.axis_index("lon")

    def lat_peer(o):
        return lax.rem(i + o + n_lat, n_lat)

    def lon_peer(o):
        return lax.rem(j + o + n_lon, n_lon)

    loads = [
        pltpu.make_async_copy(src, dst, load_sem.at[k])
        for k, (src, dst) in enumerate(
            (
                (cell_hbm, cell_ref),
                (weight_hbm, weight_ref),
                (value_hbm, value_ref),
                (sea_hbm, sea_ref),
                (coarse_hbm, coarse_ref),
                (factors_hbm, fac),
            )
        )
    ]
    for load in loads:
        load.start()

    barrier = pltpu.get_barrier_semaphore()

    def greet(pi, pj):
        pl.semaphore_signal(
            barrier, inc=1, device_id={"lat": pi, "lon": pj}, device_id_type=pl.DeviceIdType.MESH
        )

    corners = [(-1, -1), (-1, 1), (1, -1), (1, 1)]
    for o in range(1, n_lat):
        greet(lat_peer(o), j)
    for o in range(1, n_lon):
        greet(i, lon_peer(o))
    for di, dj in corners:
        greet(lat_peer(di), lon_peer(dj))

    sent = []

    def remote(src, dst, pi, pj):
        k = len(sent)
        copy = pltpu.make_async_remote_copy(
            src_ref=src,
            dst_ref=dst,
            send_sem=send_sem.at[k],
            recv_sem=recv_sem.at[k],
            device_id={"lat": pi, "lon": pj},
            device_id_type=pl.DeviceIdType.MESH,
        )
        copy.start()
        sent.append(copy)
        return copy

    for load in loads[:4]:
        load.wait()
    blank = jnp.zeros((HW, cy), F32)
    ocean = jnp.concatenate([blank, sea_ref[...].astype(F32), blank], axis=0).T
    count = cell_ref.shape[2]
    chunk = 512 if count % 512 == 0 else count
    spot_type = BF16 if max(cy, w) <= 256 else F32
    none, one = jnp.zeros((), BF16), jnp.ones((), BF16)
    sums = jnp.zeros((4 * cy, w), F32)
    for at in range(0, count, chunk):
        cell = cell_ref[0, :, at : at + chunk].astype(F32)
        row = jnp.floor((cell + 0.5) * (1.0 / cx))
        col = cell - row * cx + HW
        weight = weight_ref[0, :, at : at + chunk]
        product = weight * value_ref[0, :, at : at + chunk]
        in_row = iota((cy, chunk), 0).astype(F32).astype(spot_type) == row.astype(spot_type)
        in_col = iota((w, chunk), 0).astype(F32).astype(spot_type) == col.astype(spot_type)
        parts = []
        for x in (weight, product):
            high = x.astype(BF16)
            parts += [high, (x - high.astype(F32)).astype(BF16)]
        left = jnp.concatenate([jnp.where(in_row, x, none) for x in parts], axis=0)
        right = jnp.where(in_col, one, none)
        sums = sums + lax.dot_general(
            left, right, (((1,), (1,)), ((), ())), preferred_element_type=F32
        )
    diag[...] = sums[0:cy] + sums[cy : 2 * cy]
    rhs = ocean * (sums[2 * cy : 3 * cy] + sums[3 * cy : 4 * cy])
    core[0] = ocean
    core[1] = rhs

    block = cy // SUB
    lane_w = iota((SUB, w), 1) - HW
    sub_w = iota((SUB, w), 0) * (cx // SUB)
    group = jnp.where((lane_w >= sub_w) & (lane_w < sub_w + cx // SUB), 1.0, 0.0)
    strips = [
        jnp.sum(rhs[s * block : (s + 1) * block], axis=0, keepdims=True) * group for s in range(SUB)
    ]
    own = jnp.sum(jnp.concatenate(strips, axis=0), axis=1, keepdims=True)
    entries = SUB * SUB
    spot = iota((entries, LANES), 0) == (iota((entries, LANES), 1) % entries)
    own = jnp.sum(jnp.where(spot, own, 0.0), axis=0, keepdims=True)
    near[i] = own

    lane = iota((cy, LANES), 1)
    hi = w - LANES
    left = jnp.where(lane < QUARTER, ocean[:, :LANES], pltpu.roll(rhs[:, :LANES], HW, 1))
    right = jnp.where(lane >= LANES - HW, pltpu.roll(rhs[:, hi:], HW, 1), ocean[:, hi:])
    strips = (left, HW), (right, LANES - 2 * HW)
    for v, (x, start) in enumerate(strips):
        edge[v] = pack(x, start)
    for k, (di, dj) in enumerate(corners):
        x = strips[0 if dj < 0 else 1][0]
        corner[k] = x[0:HW] if di < 0 else x[cy - HW : cy]

    pl.semaphore_wait(barrier, n_lat - 1 + n_lon - 1 + 4)

    first = [remote(near.at[i], near.at[i], lat_peer(o), j) for o in range(1, n_lat)]
    halo = [
        remote(edge.at[0], edge_in.at[1], i, lon_peer(-1)),
        remote(edge.at[1], edge_in.at[0], i, lon_peer(1)),
        remote(core.at[:, pl.ds(0, HW)], rows_in.at[1], lat_peer(-1), j),
        remote(core.at[:, pl.ds(cy - HW, HW)], rows_in.at[0], lat_peer(1), j),
    ]
    for k, (di, dj) in enumerate(corners):
        halo.append(remote(corner.at[k], corner_in.at[3 - k], lat_peer(di), lon_peer(dj)))
    for copy in first:
        copy.wait_recv()
    per = LANES // entries
    slot = iota((1, LANES), 1) // entries
    joint = min(n_lat, per)
    for q in range(n_lat // joint):
        line = jnp.zeros((1, LANES), F32)
        for r in range(joint):
            line = jnp.where(slot % joint == r, near[q * joint + r], line)
        gather[j, q] = line
    second = [remote(gather.at[j], gather.at[j], i, lon_peer(o)) for o in range(1, n_lon)]
    for copy in halo:
        copy.wait_recv()

    def west(x):
        at = iota(x.shape, 1)
        return (
            jnp.where(at < HW, pltpu.roll(x, 2 * HW, 1), 0.0),
            jnp.where(at < HW, pltpu.roll(x, HW, 1), 0.0),
        )

    def east(x):
        at = iota(x.shape, 1)
        return (
            jnp.where(at >= LANES - HW, pltpu.roll(x, LANES - 2 * HW, 1), 0.0),
            jnp.where(at >= LANES - HW, pltpu.roll(x, LANES - 3 * HW, 1), 0.0),
        )

    spans = (
        (0, HW, rows_in.at[0], corner_in[0], corner_in[1], jnp.where(i > 0, 1.0, 0.0)),
        (HW, cy, core, unpack(edge_in[0], LANES - QUARTER), unpack(edge_in[1], HW), None),
        (HW + cy, HW, rows_in.at[1], corner_in[2], corner_in[3], jnp.where(i < n_lat - 1, 1.0, 0.0)),
    )
    for at, size, middle, left, right, inside in spans:
        for f, (lo, up) in enumerate(zip(west(left), east(right))):
            whole = middle[f]
            if inside is not None:
                whole, lo, up = whole * inside, lo * inside, up * inside
            wide[f, at : at + size, :] = whole
            wide[f, at : at + size, 0:LANES] += lo
            wide[f, at : at + size, hi:w] += up

    reach = reach_ref[0, 0]
    for load in loads[4:]:
        load.wait()
    col_pos = iota((HW, w), 1)
    col_ok = (col_pos >= HW - reach) & (col_pos < HW + cx + reach)
    blocks, size = fac.shape[0], fac.shape[1]
    for k in range(blocks):
        at = k * size
        row_pos = iota((size, w), 0) + at
        ok = col_ok & (row_pos >= HW - reach) & (row_pos < HW + cy + reach)
        scale = jnp.where(ok, wide[0, at : at + size], 0.0)
        u = scale * wide[1, at : at + size]
        g = jnp.zeros((size, w), F32)
        for p in range(size):
            row = fac[k, p]
            g = g + row * jnp.sum(row * u, axis=0, keepdims=True)
        contrib[at : at + size, :] = scale * g

    for copy in second:
        copy.wait_recv()
    answer = jnp.zeros((entries, LANES), F32)
    for k in range(n_lat * n_lon // per):
        piece = jnp.zeros((1, LANES), F32)
        for r in range(0, per, joint):
            d = k * per + r
            piece = jnp.where(slot // joint == r // joint, gather[d // n_lat, d % n_lat // joint], piece)
        answer = answer + coarse_ref[:, k * LANES : (k + 1) * LANES] * piece
    answer = jnp.sum(answer, axis=1, keepdims=True)
    for s in range(SUB):
        line = jnp.sum(answer[s * SUB : (s + 1) * SUB] * group, axis=0, keepdims=True)
        at = HW + s * block
        contrib[at : at + block, :] += core[0, s * block : (s + 1) * block, :] * line

    deep = 2 * HW
    side[0] = pack(contrib[:, 0:LANES], 0)
    side[1] = pack(contrib[:, hi:w], LANES - deep)
    for k, (di, dj) in enumerate(corners):
        top = 0 if di < 0 else h - deep
        begin, start = (0, 0) if dj < 0 else (hi, LANES - deep)
        cross[k] = pack(contrib[top : top + deep, begin : begin + LANES], start)
    back = [
        remote(side.at[0], side_in.at[1], i, lon_peer(-1)),
        remote(side.at[1], side_in.at[0], i, lon_peer(1)),
        remote(contrib.at[pl.ds(0, deep)], band_in.at[1], lat_peer(-1), j),
        remote(contrib.at[pl.ds(h - deep, deep)], band_in.at[0], lat_peer(1), j),
    ]
    for k, (di, dj) in enumerate(corners):
        back.append(remote(cross.at[k], cross_in.at[3 - k], lat_peer(di), lon_peer(dj)))
    total[...] = contrib[...]
    for copy in back:
        copy.wait_recv()

    total[:, 0:LANES] += unpack(side_in[0], 0)
    total[:, hi:w] += unpack(side_in[1], LANES - deep)
    for v in range(2):
        at = v * (h - deep)
        total[at : at + deep, :] += band_in[v]
        total[at : at + deep, 0:LANES] += unpack(cross_in[2 * v], 0)
        total[at : at + deep, hi:w] += unpack(cross_in[2 * v + 1], LANES - deep)

    p = total[HW : HW + cy, :]
    o = core[0]
    on, os = wide[0, HW - 1 : HW - 1 + cy, :], wide[0, HW + 1 : HW + 1 + cy, :]
    mid = wide[0, HW : HW + cy, :]
    oe, ow = pltpu.roll(mid, w - 1, 1), pltpu.roll(mid, 1, 1)
    beside = (
        oe * pltpu.roll(p, w - 1, 1)
        + ow * pltpu.roll(p, 1, 1)
        + on * total[HW - 1 : HW - 1 + cy, :]
        + os * total[HW + 1 : HW + 1 + cy, :]
    )
    image = o * ((diag[...] + DAMPING) * p + ((oe + ow + on + os) * p - beside)) + (1.0 - o) * p
    at = iota((cy, w), 1)
    inner = (at >= HW) & (at < HW + cx)

    def fold(x):
        x = jnp.sum(x, axis=0, keepdims=True)
        return sum(x[:, b : b + LANES] for b in range(0, w, LANES))

    mine[0:1] = fold(core[1] * p)
    mine[1:2] = fold(jnp.where(inner, p * image, 0.0))
    third = [remote(mine, lat_in.at[o - 1], lat_peer(o), j) for o in range(1, n_lat)]
    stores = []
    for k, (x, dst) in enumerate(((p, pre_hbm), (core[1], rhs_hbm), (image, image_hbm))):
        out[k] = x.T[HW : HW + cx]
        stores.append(pltpu.make_async_copy(out.at[k], dst, store_sem.at[k]))
        stores[k].start()
    partial = mine[...]
    for o in range(1, n_lat):
        third[o - 1].wait_recv()
        partial = partial + lat_in[o - 1]
    half[...] = partial
    fourth = [remote(half, lon_in.at[o - 1], i, lon_peer(o)) for o in range(1, n_lon)]
    for o in range(1, n_lon):
        fourth[o - 1].wait_recv()
        partial = partial + lon_in[o - 1]
    rho = jnp.sum(partial[0:1], axis=1, keepdims=True)
    curve = jnp.sum(partial[1:2], axis=1, keepdims=True)
    alpha_ref[...] = jnp.broadcast_to(rho / curve, alpha_ref.shape)
    for copy in sent:
        copy.wait_send()
    for store in stores:
        store.wait()


def finish(pre_ref, rhs_ref, image_ref, alpha_ref, sol_ref, res_ref, out_ref):
    alpha = alpha_ref[0:1, 0:1]
    pre = pre_ref[...]
    out_ref[...] = pre
    sol_ref[...] = alpha * pre
    res_ref[...] = rhs_ref[...] - alpha * image_ref[...]


def body(land_sea, obs_cell, obs_value, obs_weight, intersection, factors, coarse_inverse):
    n_lat, n_lon = lax.axis_size("lat"), lax.axis_size("lon")
    cy, cx = land_sea.shape
    h, w = cy + 2 * HW, cx + 2 * HW
    copies = 2 * (n_lat - 1 + n_lon - 1) + 16
    vmem = pl.BlockSpec(memory_space=pltpu.VMEM)
    entries = SUB * SUB
    lines = n_lat // min(n_lat, LANES // entries)
    hbm = pl.BlockSpec(memory_space=pltpu.HBM)
    out = jax.ShapeDtypeStruct((cx, cy), F32)
    fields = pl.pallas_call(
        functools.partial(kernel, n_lat, n_lon),
        out_shape=(out, out, out, jax.ShapeDtypeStruct((8, LANES), F32)),
        in_specs=[hbm, hbm, hbm, hbm, pl.BlockSpec(memory_space=pltpu.SMEM), hbm, hbm],
        out_specs=(hbm, hbm, hbm, vmem),
        scratch_shapes=[
            pltpu.VMEM((cx, cy), jnp.int32),
            pltpu.VMEM(obs_cell.shape, jnp.int32),
            pltpu.VMEM(obs_value.shape, F32),
            pltpu.VMEM(obs_weight.shape, F32),
            pltpu.VMEM(factors.shape, F32),
            pltpu.VMEM(coarse_inverse.shape, F32),
            pltpu.VMEM((cy, w), F32),
            pltpu.VMEM((2, cy, w), F32),
            pltpu.VMEM((2, h, w), F32),
            pltpu.VMEM((2, cy // 4, LANES), F32),
            pltpu.VMEM((2, cy // 4, LANES), F32),
            pltpu.VMEM((4, HW, LANES), F32),
            pltpu.VMEM((2, 2, HW, w), F32),
            pltpu.VMEM((4, HW, LANES), F32),
            pltpu.VMEM((n_lat, 1, LANES), F32),
            pltpu.VMEM((n_lon, lines, 1, LANES), F32),
            pltpu.VMEM((h, w), F32),
            pltpu.VMEM((2, h // 4, LANES), F32),
            pltpu.VMEM((2, h // 4, LANES), F32),
            pltpu.VMEM((2, 2 * HW, w), F32),
            pltpu.VMEM((4, HW // 2, LANES), F32),
            pltpu.VMEM((4, HW // 2, LANES), F32),
            pltpu.VMEM((h, w), F32),
            pltpu.VMEM((2, LANES), F32),
            pltpu.VMEM((n_lat - 1, 2, LANES), F32),
            pltpu.VMEM((2, LANES), F32),
            pltpu.VMEM((n_lon - 1, 2, LANES), F32),
            pltpu.VMEM((3, cx, cy), F32),
            pltpu.SemaphoreType.DMA((6,)),
            pltpu.SemaphoreType.DMA((3,)),
            pltpu.SemaphoreType.DMA((copies,)),
            pltpu.SemaphoreType.DMA((copies,)),
        ],
        compiler_params=pltpu.CompilerParams(
            collective_id=0, has_side_effects=True, vmem_limit_bytes=64 * 1024 * 1024
        ),
    )(land_sea.T, obs_cell, obs_value, obs_weight, intersection, factors, coarse_inverse)
    results = pl.pallas_call(
        finish,
        out_shape=(out, out, out),
        in_specs=[vmem] * 4,
        out_specs=(vmem, vmem, vmem),
        compiler_params=pltpu.CompilerParams(vmem_limit_bytes=64 * 1024 * 1024),
    )(*fields)
    return tuple(x.T for x in results)


def solution(mesh):
    in_specs = (
        P("lat", "lon"),
        P("lat", "lon", None),
        P("lat", "lon", None),
        P("lat", "lon", None),
        P("lat", "lon"),
        P("lat", None, None, "lon"),
        P(("lon", "lat"), None),
    )
    out_specs = (P("lat", "lon"), P("lat", "lon"), P("lat", "lon"))
    return jax.shard_map(body, mesh=mesh, in_specs=in_specs, out_specs=out_specs, check_vma=False)
```

```python
import functools

import jax
import jax.numpy as jnp
from jax import lax
from jax.experimental import pallas as pl
from jax.experimental.pallas import tpu as pltpu
from jax.sharding import PartitionSpec as P

HW = 16
SUB = 4
DAMPING = 0.02
DIRECT = 64
LANES = 128
F32 = jnp.float32
BF16 = jnp.bfloat16


def iota(shape, dim):
    return lax.broadcasted_iota(jnp.int32, shape, dim)


QUARTER = 2 * HW


def pack(x, start):
    groups = LANES // QUARTER
    size = x.shape[0] // groups
    at = iota((size, LANES), 1) // QUARTER
    whole = jnp.zeros((size, LANES), F32)
    for g in range(groups):
        part = x[g * size : (g + 1) * size]
        shift = (g * QUARTER - start) % LANES
        part = pltpu.roll(part, shift, 1) if shift else part
        whole = jnp.where(at == g, part, whole)
    return whole


def unpack(x, start):
    groups = LANES // QUARTER
    at = iota(x.shape, 1)
    parts = []
    for g in range(groups):
        shift = (start - g * QUARTER) % LANES
        part = pltpu.roll(x, shift, 1) if shift else x
        parts.append(jnp.where((at >= start) & (at < start + QUARTER), part, 0.0))
    return jnp.concatenate(parts, axis=0)


def kernel(
    n_lat, n_lon,
    sea_hbm, cell_hbm, value_hbm, weight_hbm, reach_ref, factors_hbm, coarse_hbm,
    pre_hbm, rhs_hbm, image_hbm, alpha_ref,
    sea_ref, cell_ref, value_ref, weight_ref, fac, coarse_ref,
    diag, core, wide, edge, edge_in, corner, rows_in, corner_in, near, gather,
    contrib, side, side_in, band_in, cross, cross_in, total, mine, lat_in, half, lon_in, out,
    load_sem, store_sem, send_sem, recv_sem,
):
    cx, cy = sea_ref.shape
    h, w = cy + 2 * HW, cx + 2 * HW
    i, j = lax.axis_index("lat"), lax.axis_index("lon")

    def lat_peer(o):
        return lax.rem(i + o + n_lat, n_lat)

    def lon_peer(o):
        return lax.rem(j + o + n_lon, n_lon)

    loads = [
        pltpu.make_async_copy(src, dst, load_sem.at[k])
        for k, (src, dst) in enumerate(
            (
                (cell_hbm, cell_ref),
                (weight_hbm, weight_ref),
                (value_hbm, value_ref),
                (sea_hbm, sea_ref),
                (coarse_hbm, coarse_ref),
                (factors_hbm, fac),
            )
        )
    ]
    for load in loads:
        load.start()

    barrier = pltpu.get_barrier_semaphore()

    def greet(pi, pj):
        pl.semaphore_signal(
            barrier, inc=1, device_id={"lat": pi, "lon": pj}, device_id_type=pl.DeviceIdType.MESH
        )

    corners = [(-1, -1), (-1, 1), (1, -1), (1, 1)]
    others = [(a, b) for a in range(n_lat) for b in range(n_lon) if a or b]
    direct = len(others) < DIRECT
    if direct:
        for a, b in others:
            greet(lat_peer(a), lon_peer(b))
    else:
        for o in range(1, n_lat):
            greet(lat_peer(o), j)
        for o in range(1, n_lon):
            greet(i, lon_peer(o))
        for di, dj in corners:
            greet(lat_peer(di), lon_peer(dj))

    used = [0]

    def remote(src, dst, pi, pj):
        k = used[0]
        used[0] += 1
        copy = pltpu.make_async_remote_copy(
            src_ref=src,
            dst_ref=dst,
            send_sem=send_sem.at[k],
            recv_sem=recv_sem.at[k],
            device_id={"lat": pi, "lon": pj},
            device_id_type=pl.DeviceIdType.MESH,
        )
        copy.start()
        return copy

    for load in loads[:4]:
        load.wait()
    blank = jnp.zeros((HW, cy), F32)
    ocean = jnp.concatenate([blank, sea_ref[...].astype(F32), blank], axis=0).T
    count = cell_ref.shape[2]
    chunk = 512 if count % 512 == 0 else count
    sums = jnp.zeros((4 * cy, w), F32)
    for at in range(0, count, chunk):
        cell = cell_ref[0, :, at : at + chunk].astype(F32)
        row = jnp.floor((cell + 0.5) * (1.0 / cx))
        col = cell - row * cx + HW
        weight = weight_ref[0, :, at : at + chunk]
        product = weight * value_ref[0, :, at : at + chunk]
        in_row = iota((cy, chunk), 0).astype(F32) == row
        in_col = iota((w, chunk), 0).astype(F32) == col
        parts = []
        for x in (weight, product):
            high = x.astype(BF16).astype(F32)
            parts += [high, x - high]
        left = jnp.concatenate([jnp.where(in_row, x, 0.0).astype(BF16) for x in parts], axis=0)
        right = jnp.where(in_col, 1.0, 0.0).astype(BF16)
        sums = sums + lax.dot_general(
            left, right, (((1,), (1,)), ((), ())), preferred_element_type=F32
        )
    diag[...] = sums[0:cy] + sums[cy : 2 * cy]
    rhs = ocean * (sums[2 * cy : 3 * cy] + sums[3 * cy : 4 * cy])
    core[0] = ocean
    core[1] = rhs

    block = cy // SUB
    lane_w = iota((SUB, w), 1) - HW
    sub_w = iota((SUB, w), 0) * (cx // SUB)
    group = jnp.where((lane_w >= sub_w) & (lane_w < sub_w + cx // SUB), 1.0, 0.0)
    strips = [
        jnp.sum(rhs[s * block : (s + 1) * block], axis=0, keepdims=True) * group for s in range(SUB)
    ]
    own = jnp.sum(jnp.concatenate(strips, axis=0), axis=1, keepdims=True)
    entries = SUB * SUB
    spot = iota((entries, LANES), 0) == (iota((entries, LANES), 1) % entries)
    own = jnp.sum(jnp.where(spot, own, 0.0), axis=0, keepdims=True)
    near[i] = own

    lane = iota((cy, LANES), 1)
    hi = w - LANES
    left = jnp.where(lane < QUARTER, ocean[:, :LANES], pltpu.roll(rhs[:, :LANES], HW, 1))
    right = jnp.where(lane >= LANES - HW, pltpu.roll(rhs[:, hi:], HW, 1), ocean[:, hi:])
    strips = (left, HW), (right, LANES - 2 * HW)
    for v, (x, start) in enumerate(strips):
        edge[v] = pack(x, start)
    for k, (di, dj) in enumerate(corners):
        x = strips[0 if dj < 0 else 1][0]
        corner[k] = x[0:HW] if di < 0 else x[cy - HW : cy]

    pl.semaphore_wait(barrier, len(others) if direct else n_lat - 1 + n_lon - 1 + 4)

    first = [remote(near.at[i], near.at[i], lat_peer(o), j) for o in range(1, n_lat)]
    halo = [
        remote(edge.at[0], edge_in.at[1], i, lon_peer(-1)),
        remote(edge.at[1], edge_in.at[0], i, lon_peer(1)),
        remote(core.at[:, pl.ds(0, HW)], rows_in.at[1], lat_peer(-1), j),
        remote(core.at[:, pl.ds(cy - HW, HW)], rows_in.at[0], lat_peer(1), j),
    ]
    for k, (di, dj) in enumerate(corners):
        halo.append(remote(corner.at[k], corner_in.at[3 - k], lat_peer(di), lon_peer(dj)))
    for copy in first:
        copy.wait()
    per = LANES // entries
    slot = iota((1, LANES), 1) // entries
    joint = min(n_lat, per)
    for q in range(n_lat // joint):
        line = jnp.zeros((1, LANES), F32)
        for r in range(joint):
            line = jnp.where(slot % joint == r, near[q * joint + r], line)
        gather[j, q] = line
    second = [remote(gather.at[j], gather.at[j], i, lon_peer(o)) for o in range(1, n_lon)]
    for copy in halo:
        copy.wait()

    def west(x):
        at = iota(x.shape, 1)
        return (
            jnp.where(at < HW, pltpu.roll(x, 2 * HW, 1), 0.0),
            jnp.where(at < HW, pltpu.roll(x, HW, 1), 0.0),
        )

    def east(x):
        at = iota(x.shape, 1)
        return (
            jnp.where(at >= LANES - HW, pltpu.roll(x, LANES - 2 * HW, 1), 0.0),
            jnp.where(at >= LANES - HW, pltpu.roll(x, LANES - 3 * HW, 1), 0.0),
        )

    spans = (
        (0, HW, rows_in.at[0], corner_in[0], corner_in[1], jnp.where(i > 0, 1.0, 0.0)),
        (HW, cy, core, unpack(edge_in[0], LANES - QUARTER), unpack(edge_in[1], HW), None),
        (HW + cy, HW, rows_in.at[1], corner_in[2], corner_in[3], jnp.where(i < n_lat - 1, 1.0, 0.0)),
    )
    for at, size, middle, left, right, inside in spans:
        for f, (lo, up) in enumerate(zip(west(left), east(right))):
            whole = middle[f]
            if inside is not None:
                whole, lo, up = whole * inside, lo * inside, up * inside
            wide[f, at : at + size, :] = whole
            wide[f, at : at + size, 0:LANES] += lo
            wide[f, at : at + size, hi:w] += up

    reach = reach_ref[0, 0]
    for load in loads[4:]:
        load.wait()
    col_pos = iota((HW, w), 1)
    col_ok = (col_pos >= HW - reach) & (col_pos < HW + cx + reach)
    blocks, size = fac.shape[0], fac.shape[1]
    for k in range(blocks):
        at = k * size
        row_pos = iota((size, w), 0) + at
        ok = col_ok & (row_pos >= HW - reach) & (row_pos < HW + cy + reach)
        scale = jnp.where(ok, wide[0, at : at + size], 0.0)
        u = scale * wide[1, at : at + size]
        g = jnp.zeros((size, w), F32)
        for p in range(size):
            row = fac[k, p]
            g = g + row * jnp.sum(row * u, axis=0, keepdims=True)
        contrib[at : at + size, :] = scale * g

    for copy in second:
        copy.wait()
    answer = jnp.zeros((entries, LANES), F32)
    for k in range(n_lat * n_lon // per):
        piece = jnp.zeros((1, LANES), F32)
        for r in range(0, per, joint):
            d = k * per + r
            piece = jnp.where(slot // joint == r // joint, gather[d // n_lat, d % n_lat // joint], piece)
        answer = answer + coarse_ref[:, k * LANES : (k + 1) * LANES] * piece
    answer = jnp.sum(answer, axis=1, keepdims=True)
    for s in range(SUB):
        line = jnp.sum(answer[s * SUB : (s + 1) * SUB] * group, axis=0, keepdims=True)
        at = HW + s * block
        contrib[at : at + block, :] += core[0, s * block : (s + 1) * block, :] * line

    deep = 2 * HW
    side[0] = pack(contrib[:, 0:LANES], 0)
    side[1] = pack(contrib[:, hi:w], LANES - deep)
    for k, (di, dj) in enumerate(corners):
        top = 0 if di < 0 else h - deep
        begin, start = (0, 0) if dj < 0 else (hi, LANES - deep)
        cross[k] = pack(contrib[top : top + deep, begin : begin + LANES], start)
    back = [
        remote(side.at[0], side_in.at[1], i, lon_peer(-1)),
        remote(side.at[1], side_in.at[0], i, lon_peer(1)),
        remote(contrib.at[pl.ds(0, deep)], band_in.at[1], lat_peer(-1), j),
        remote(contrib.at[pl.ds(h - deep, deep)], band_in.at[0], lat_peer(1), j),
    ]
    for k, (di, dj) in enumerate(corners):
        back.append(remote(cross.at[k], cross_in.at[3 - k], lat_peer(di), lon_peer(dj)))
    total[...] = contrib[...]
    for copy in back:
        copy.wait()

    total[:, 0:LANES] += unpack(side_in[0], 0)
    total[:, hi:w] += unpack(side_in[1], LANES - deep)
    for v in range(2):
        at = v * (h - deep)
        total[at : at + deep, :] += band_in[v]
        total[at : at + deep, 0:LANES] += unpack(cross_in[2 * v], 0)
        total[at : at + deep, hi:w] += unpack(cross_in[2 * v + 1], LANES - deep)

    p = total[HW : HW + cy, :]
    o = core[0]
    on, os = wide[0, HW - 1 : HW - 1 + cy, :], wide[0, HW + 1 : HW + 1 + cy, :]
    mid = wide[0, HW : HW + cy, :]
    oe, ow = pltpu.roll(mid, w - 1, 1), pltpu.roll(mid, 1, 1)
    beside = (
        oe * pltpu.roll(p, w - 1, 1)
        + ow * pltpu.roll(p, 1, 1)
        + on * total[HW - 1 : HW - 1 + cy, :]
        + os * total[HW + 1 : HW + 1 + cy, :]
    )
    image = o * ((diag[...] + DAMPING) * p + ((oe + ow + on + os) * p - beside)) + (1.0 - o) * p
    at = iota((cy, w), 1)
    inner = (at >= HW) & (at < HW + cx)

    def fold(x):
        x = jnp.sum(x, axis=0, keepdims=True)
        return sum(x[:, b : b + LANES] for b in range(0, w, LANES))

    mine[0:1] = fold(core[1] * p)
    mine[1:2] = fold(jnp.where(inner, p * image, 0.0))
    if direct:
        third = [
            remote(mine, lon_in.at[k], lat_peer(a), lon_peer(b)) for k, (a, b) in enumerate(others)
        ]
    else:
        third = [remote(mine, lat_in.at[o - 1], lat_peer(o), j) for o in range(1, n_lat)]
    stores = []
    for k, (x, dst) in enumerate(((p, pre_hbm), (core[1], rhs_hbm), (image, image_hbm))):
        out[k] = x.T[HW : HW + cx]
        stores.append(pltpu.make_async_copy(out.at[k], dst, store_sem.at[k]))
        stores[k].start()
    partial = mine[...]
    if direct:
        for k, copy in enumerate(third):
            copy.wait_recv()
            partial = partial + lon_in[k]
    else:
        for k, copy in enumerate(third):
            copy.wait_recv()
            partial = partial + lat_in[k]
        half[...] = partial
        fourth = [remote(half, lon_in.at[o - 1], i, lon_peer(o)) for o in range(1, n_lon)]
        for k, copy in enumerate(fourth):
            copy.wait_recv()
            partial = partial + lon_in[k]
        third = third + fourth
    rho = jnp.sum(partial[0:1], axis=1, keepdims=True)
    curve = jnp.sum(partial[1:2], axis=1, keepdims=True)
    alpha_ref[...] = jnp.broadcast_to(rho / curve, alpha_ref.shape)
    for copy in third:
        copy.wait_send()
    for store in stores:
        store.wait()


def finish(pre_ref, rhs_ref, image_ref, alpha_ref, sol_ref, res_ref, out_ref):
    alpha = alpha_ref[0:1, 0:1]
    pre = pre_ref[...]
    out_ref[...] = pre
    sol_ref[...] = alpha * pre
    res_ref[...] = rhs_ref[...] - alpha * image_ref[...]


def body(land_sea, obs_cell, obs_value, obs_weight, intersection, factors, coarse_inverse):
    n_lat, n_lon = lax.axis_size("lat"), lax.axis_size("lon")
    cy, cx = land_sea.shape
    h, w = cy + 2 * HW, cx + 2 * HW
    others = n_lat * n_lon - 1
    sums = others if others < DIRECT else n_lon - 1
    copies = 2 * (n_lat - 1) + n_lon - 1 + sums + 16
    vmem = pl.BlockSpec(memory_space=pltpu.VMEM)
    entries = SUB * SUB
    lines = n_lat // min(n_lat, LANES // entries)
    hbm = pl.BlockSpec(memory_space=pltpu.HBM)
    out = jax.ShapeDtypeStruct((cx, cy), F32)
    fields = pl.pallas_call(
        functools.partial(kernel, n_lat, n_lon),
        out_shape=(out, out, out, jax.ShapeDtypeStruct((8, LANES), F32)),
        in_specs=[hbm, hbm, hbm, hbm, pl.BlockSpec(memory_space=pltpu.SMEM), hbm, hbm],
        out_specs=(hbm, hbm, hbm, vmem),
        scratch_shapes=[
            pltpu.VMEM((cx, cy), jnp.int32),
            pltpu.VMEM(obs_cell.shape, jnp.int32),
            pltpu.VMEM(obs_value.shape, F32),
            pltpu.VMEM(obs_weight.shape, F32),
            pltpu.VMEM(factors.shape, F32),
            pltpu.VMEM(coarse_inverse.shape, F32),
            pltpu.VMEM((cy, w), F32),
            pltpu.VMEM((2, cy, w), F32),
            pltpu.VMEM((2, h, w), F32),
            pltpu.VMEM((2, cy // 4, LANES), F32),
            pltpu.VMEM((2, cy // 4, LANES), F32),
            pltpu.VMEM((4, HW, LANES), F32),
            pltpu.VMEM((2, 2, HW, w), F32),
            pltpu.VMEM((4, HW, LANES), F32),
            pltpu.VMEM((n_lat, 1, LANES), F32),
            pltpu.VMEM((n_lon, lines, 1, LANES), F32),
            pltpu.VMEM((h, w), F32),
            pltpu.VMEM((2, h // 4, LANES), F32),
            pltpu.VMEM((2, h // 4, LANES), F32),
            pltpu.VMEM((2, 2 * HW, w), F32),
            pltpu.VMEM((4, HW // 2, LANES), F32),
            pltpu.VMEM((4, HW // 2, LANES), F32),
            pltpu.VMEM((h, w), F32),
            pltpu.VMEM((2, LANES), F32),
            pltpu.VMEM((n_lat - 1, 2, LANES), F32),
            pltpu.VMEM((2, LANES), F32),
            pltpu.VMEM((sums, 2, LANES), F32),
            pltpu.VMEM((3, cx, cy), F32),
            pltpu.SemaphoreType.DMA((6,)),
            pltpu.SemaphoreType.DMA((3,)),
            pltpu.SemaphoreType.DMA((copies,)),
            pltpu.SemaphoreType.DMA((copies,)),
        ],
        compiler_params=pltpu.CompilerParams(
            collective_id=0, has_side_effects=True, vmem_limit_bytes=64 * 1024 * 1024
        ),
    )(land_sea.T, obs_cell, obs_value, obs_weight, intersection, factors, coarse_inverse)
    results = pl.pallas_call(
        finish,
        out_shape=(out, out, out),
        in_specs=[vmem] * 4,
        out_specs=(vmem, vmem, vmem),
        compiler_params=pltpu.CompilerParams(vmem_limit_bytes=64 * 1024 * 1024),
    )(*fields)
    return tuple(x.T for x in results)


def solution(mesh):
    in_specs = (
        P("lat", "lon"),
        P("lat", "lon", None),
        P("lat", "lon", None),
        P("lat", "lon", None),
        P("lat", "lon"),
        P("lat", None, None, "lon"),
        P(("lon", "lat"), None),
    )
    out_specs = (P("lat", "lon"), P("lat", "lon"), P("lat", "lon"))
    return jax.shard_map(body, mesh=mesh, in_specs=in_specs, out_specs=out_specs, check_vma=False)
```

```python
import functools

import jax
import jax.numpy as jnp
from jax import lax
from jax.experimental import pallas as pl
from jax.experimental.pallas import tpu as pltpu
from jax.sharding import PartitionSpec as P

HW = 16
SUB = 4
DAMPING = 0.02
DIRECT = 64
LANES = 128
F32 = jnp.float32
BF16 = jnp.bfloat16


def iota(shape, dim):
    return lax.broadcasted_iota(jnp.int32, shape, dim)


QUARTER = 2 * HW


def pack(x, start):
    groups = LANES // QUARTER
    size = x.shape[0] // groups
    at = iota((size, LANES), 1) // QUARTER
    whole = jnp.zeros((size, LANES), F32)
    for g in range(groups):
        part = x[g * size : (g + 1) * size]
        shift = (g * QUARTER - start) % LANES
        part = pltpu.roll(part, shift, 1) if shift else part
        whole = jnp.where(at == g, part, whole)
    return whole


def unpack(x, start):
    groups = LANES // QUARTER
    at = iota(x.shape, 1)
    parts = []
    for g in range(groups):
        shift = (start - g * QUARTER) % LANES
        part = pltpu.roll(x, shift, 1) if shift else x
        parts.append(jnp.where((at >= start) & (at < start + QUARTER), part, 0.0))
    return jnp.concatenate(parts, axis=0)


def kernel(
    n_lat, n_lon,
    sea_hbm, cell_hbm, value_hbm, weight_hbm, reach_ref, factors_hbm, coarse_hbm,
    pre_hbm, rhs_hbm, image_hbm, alpha_ref,
    sea_ref, cell_ref, value_ref, weight_ref, fac, coarse_ref,
    diag, core, wide, edge, edge_in, corner, rows_in, corner_in, near, gather,
    contrib, side, side_in, band_in, cross, cross_in, total, mine, lat_in, half, lon_in, out,
    load_sem, store_sem, send_sem, recv_sem,
):
    cx, cy = sea_ref.shape
    h, w = cy + 2 * HW, cx + 2 * HW
    i, j = lax.axis_index("lat"), lax.axis_index("lon")

    def lat_peer(o):
        return lax.rem(i + o + n_lat, n_lat)

    def lon_peer(o):
        return lax.rem(j + o + n_lon, n_lon)

    loads = [
        pltpu.make_async_copy(src, dst, load_sem.at[k])
        for k, (src, dst) in enumerate(
            (
                (cell_hbm, cell_ref),
                (weight_hbm, weight_ref),
                (value_hbm, value_ref),
                (sea_hbm, sea_ref),
                (coarse_hbm, coarse_ref),
                (factors_hbm, fac),
            )
        )
    ]
    for load in loads:
        load.start()

    barrier = pltpu.get_barrier_semaphore()

    def greet(pi, pj):
        pl.semaphore_signal(
            barrier, inc=1, device_id={"lat": pi, "lon": pj}, device_id_type=pl.DeviceIdType.MESH
        )

    corners = [(-1, -1), (-1, 1), (1, -1), (1, 1)]
    others = [(a, b) for a in range(n_lat) for b in range(n_lon) if a or b]
    direct = len(others) < DIRECT
    if direct:
        for a, b in others:
            greet(lat_peer(a), lon_peer(b))
    else:
        for o in range(1, n_lat):
            greet(lat_peer(o), j)
        for o in range(1, n_lon):
            greet(i, lon_peer(o))
        for di, dj in corners:
            greet(lat_peer(di), lon_peer(dj))

    used = [0]

    def remote(src, dst, pi, pj):
        k = used[0]
        used[0] += 1
        copy = pltpu.make_async_remote_copy(
            src_ref=src,
            dst_ref=dst,
            send_sem=send_sem.at[k],
            recv_sem=recv_sem.at[k],
            device_id={"lat": pi, "lon": pj},
            device_id_type=pl.DeviceIdType.MESH,
        )
        copy.start()
        return copy

    for load in loads[:4]:
        load.wait()
    blank = jnp.zeros((HW, cy), F32)
    ocean = jnp.concatenate([blank, sea_ref[...].astype(F32), blank], axis=0).T
    count = cell_ref.shape[2]
    chunk = 1024 if count % 1024 == 0 else count
    sums = jnp.zeros((4 * cy, w), F32)
    for at in range(0, count, chunk):
        cell = cell_ref[0, :, at : at + chunk].astype(F32)
        row = jnp.floor((cell + 0.5) * (1.0 / cx))
        col = cell - row * cx + HW
        weight = weight_ref[0, :, at : at + chunk]
        product = weight * value_ref[0, :, at : at + chunk]
        in_row = iota((cy, chunk), 0).astype(F32) == row
        in_col = iota((w, chunk), 0).astype(F32) == col
        parts = []
        for x in (weight, product):
            high = x.astype(BF16).astype(F32)
            parts += [high, x - high]
        left = jnp.concatenate([jnp.where(in_row, x, 0.0).astype(BF16) for x in parts], axis=0)
        right = jnp.where(in_col, 1.0, 0.0).astype(BF16)
        sums = sums + lax.dot_general(
            left, right, (((1,), (1,)), ((), ())), preferred_element_type=F32
        )
    diag[...] = sums[0:cy] + sums[cy : 2 * cy]
    rhs = ocean * (sums[2 * cy : 3 * cy] + sums[3 * cy : 4 * cy])
    core[0] = ocean
    core[1] = rhs

    block = cy // SUB
    lane_w = iota((SUB, w), 1) - HW
    sub_w = iota((SUB, w), 0) * (cx // SUB)
    group = jnp.where((lane_w >= sub_w) & (lane_w < sub_w + cx // SUB), 1.0, 0.0)
    strips = [
        jnp.sum(rhs[s * block : (s + 1) * block], axis=0, keepdims=True) * group for s in range(SUB)
    ]
    own = jnp.sum(jnp.concatenate(strips, axis=0), axis=1, keepdims=True)
    entries = SUB * SUB
    spot = iota((entries, LANES), 0) == (iota((entries, LANES), 1) % entries)
    own = jnp.sum(jnp.where(spot, own, 0.0), axis=0, keepdims=True)
    near[i] = own

    lane = iota((cy, LANES), 1)
    hi = w - LANES
    left = jnp.where(lane < QUARTER, ocean[:, :LANES], pltpu.roll(rhs[:, :LANES], HW, 1))
    right = jnp.where(lane >= LANES - HW, pltpu.roll(rhs[:, hi:], HW, 1), ocean[:, hi:])
    strips = (left, HW), (right, LANES - 2 * HW)
    for v, (x, start) in enumerate(strips):
        edge[v] = pack(x, start)
    for k, (di, dj) in enumerate(corners):
        x = strips[0 if dj < 0 else 1][0]
        corner[k] = x[0:HW] if di < 0 else x[cy - HW : cy]

    pl.semaphore_wait(barrier, len(others) if direct else n_lat - 1 + n_lon - 1 + 4)

    first = [remote(near.at[i], near.at[i], lat_peer(o), j) for o in range(1, n_lat)]
    halo = [
        remote(edge.at[0], edge_in.at[1], i, lon_peer(-1)),
        remote(edge.at[1], edge_in.at[0], i, lon_peer(1)),
        remote(core.at[:, pl.ds(0, HW)], rows_in.at[1], lat_peer(-1), j),
        remote(core.at[:, pl.ds(cy - HW, HW)], rows_in.at[0], lat_peer(1), j),
    ]
    for k, (di, dj) in enumerate(corners):
        halo.append(remote(corner.at[k], corner_in.at[3 - k], lat_peer(di), lon_peer(dj)))
    for copy in first:
        copy.wait()
    per = LANES // entries
    slot = iota((1, LANES), 1) // entries
    joint = min(n_lat, per)
    for q in range(n_lat // joint):
        line = jnp.zeros((1, LANES), F32)
        for r in range(joint):
            line = jnp.where(slot % joint == r, near[q * joint + r], line)
        gather[j, q] = line
    second = [remote(gather.at[j], gather.at[j], i, lon_peer(o)) for o in range(1, n_lon)]
    for copy in halo:
        copy.wait()

    def west(x):
        at = iota(x.shape, 1)
        return (
            jnp.where(at < HW, pltpu.roll(x, 2 * HW, 1), 0.0),
            jnp.where(at < HW, pltpu.roll(x, HW, 1), 0.0),
        )

    def east(x):
        at = iota(x.shape, 1)
        return (
            jnp.where(at >= LANES - HW, pltpu.roll(x, LANES - 2 * HW, 1), 0.0),
            jnp.where(at >= LANES - HW, pltpu.roll(x, LANES - 3 * HW, 1), 0.0),
        )

    spans = (
        (0, HW, rows_in.at[0], corner_in[0], corner_in[1], jnp.where(i > 0, 1.0, 0.0)),
        (HW, cy, core, unpack(edge_in[0], LANES - QUARTER), unpack(edge_in[1], HW), None),
        (HW + cy, HW, rows_in.at[1], corner_in[2], corner_in[3], jnp.where(i < n_lat - 1, 1.0, 0.0)),
    )
    for at, size, middle, left, right, inside in spans:
        for f, (lo, up) in enumerate(zip(west(left), east(right))):
            whole = middle[f]
            if inside is not None:
                whole, lo, up = whole * inside, lo * inside, up * inside
            wide[f, at : at + size, :] = whole
            wide[f, at : at + size, 0:LANES] += lo
            wide[f, at : at + size, hi:w] += up

    reach = reach_ref[0, 0]
    for load in loads[4:]:
        load.wait()
    col_pos = iota((HW, w), 1)
    col_ok = (col_pos >= HW - reach) & (col_pos < HW + cx + reach)
    blocks, size = fac.shape[0], fac.shape[1]
    for k in range(blocks):
        at = k * size
        row_pos = iota((size, w), 0) + at
        ok = col_ok & (row_pos >= HW - reach) & (row_pos < HW + cy + reach)
        scale = jnp.where(ok, wide[0, at : at + size], 0.0)
        u = scale * wide[1, at : at + size]
        g = jnp.zeros((size, w), F32)
        for p in range(size):
            row = fac[k, p]
            g = g + row * jnp.sum(row * u, axis=0, keepdims=True)
        contrib[at : at + size, :] = scale * g

    for copy in second:
        copy.wait()
    answer = jnp.zeros((entries, LANES), F32)
    for k in range(n_lat * n_lon // per):
        piece = jnp.zeros((1, LANES), F32)
        for r in range(0, per, joint):
            d = k * per + r
            piece = jnp.where(slot // joint == r // joint, gather[d // n_lat, d % n_lat // joint], piece)
        answer = answer + coarse_ref[:, k * LANES : (k + 1) * LANES] * piece
    answer = jnp.sum(answer, axis=1, keepdims=True)
    for s in range(SUB):
        line = jnp.sum(answer[s * SUB : (s + 1) * SUB] * group, axis=0, keepdims=True)
        at = HW + s * block
        contrib[at : at + block, :] += core[0, s * block : (s + 1) * block, :] * line

    deep = 2 * HW
    side[0] = pack(contrib[:, 0:LANES], 0)
    side[1] = pack(contrib[:, hi:w], LANES - deep)
    for k, (di, dj) in enumerate(corners):
        top = 0 if di < 0 else h - deep
        begin, start = (0, 0) if dj < 0 else (hi, LANES - deep)
        cross[k] = pack(contrib[top : top + deep, begin : begin + LANES], start)
    back = [
        remote(side.at[0], side_in.at[1], i, lon_peer(-1)),
        remote(side.at[1], side_in.at[0], i, lon_peer(1)),
        remote(contrib.at[pl.ds(0, deep)], band_in.at[1], lat_peer(-1), j),
        remote(contrib.at[pl.ds(h - deep, deep)], band_in.at[0], lat_peer(1), j),
    ]
    for k, (di, dj) in enumerate(corners):
        back.append(remote(cross.at[k], cross_in.at[3 - k], lat_peer(di), lon_peer(dj)))
    total[...] = contrib[...]
    for copy in back:
        copy.wait()

    total[:, 0:LANES] += unpack(side_in[0], 0)
    total[:, hi:w] += unpack(side_in[1], LANES - deep)
    for v in range(2):
        at = v * (h - deep)
        total[at : at + deep, :] += band_in[v]
        total[at : at + deep, 0:LANES] += unpack(cross_in[2 * v], 0)
        total[at : at + deep, hi:w] += unpack(cross_in[2 * v + 1], LANES - deep)

    p = total[HW : HW + cy, :]
    o = core[0]
    on, os = wide[0, HW - 1 : HW - 1 + cy, :], wide[0, HW + 1 : HW + 1 + cy, :]
    mid = wide[0, HW : HW + cy, :]
    oe, ow = pltpu.roll(mid, w - 1, 1), pltpu.roll(mid, 1, 1)
    beside = (
        oe * pltpu.roll(p, w - 1, 1)
        + ow * pltpu.roll(p, 1, 1)
        + on * total[HW - 1 : HW - 1 + cy, :]
        + os * total[HW + 1 : HW + 1 + cy, :]
    )
    image = o * ((diag[...] + DAMPING) * p + ((oe + ow + on + os) * p - beside)) + (1.0 - o) * p
    at = iota((cy, w), 1)
    inner = (at >= HW) & (at < HW + cx)

    def fold(x):
        x = jnp.sum(x, axis=0, keepdims=True)
        return sum(x[:, b : b + LANES] for b in range(0, w, LANES))

    mine[0:1] = fold(core[1] * p)
    mine[1:2] = fold(jnp.where(inner, p * image, 0.0))
    if direct:
        third = [
            remote(mine, lon_in.at[k], lat_peer(a), lon_peer(b)) for k, (a, b) in enumerate(others)
        ]
    else:
        third = [remote(mine, lat_in.at[o - 1], lat_peer(o), j) for o in range(1, n_lat)]
    stores = []
    for k, (x, dst) in enumerate(((p, pre_hbm), (core[1], rhs_hbm), (image, image_hbm))):
        out[k] = x.T[HW : HW + cx]
        stores.append(pltpu.make_async_copy(out.at[k], dst, store_sem.at[k]))
        stores[k].start()
    partial = mine[...]
    if direct:
        for k, copy in enumerate(third):
            copy.wait_recv()
            partial = partial + lon_in[k]
    else:
        for k, copy in enumerate(third):
            copy.wait_recv()
            partial = partial + lat_in[k]
        half[...] = partial
        fourth = [remote(half, lon_in.at[o - 1], i, lon_peer(o)) for o in range(1, n_lon)]
        for k, copy in enumerate(fourth):
            copy.wait_recv()
            partial = partial + lon_in[k]
        third = third + fourth
    rho = jnp.sum(partial[0:1], axis=1, keepdims=True)
    curve = jnp.sum(partial[1:2], axis=1, keepdims=True)
    alpha_ref[...] = jnp.broadcast_to(rho / curve, alpha_ref.shape)
    for copy in third:
        copy.wait_send()
    for store in stores:
        store.wait()


def finish(pre_ref, rhs_ref, image_ref, alpha_ref, sol_ref, res_ref, out_ref):
    alpha = alpha_ref[0:1, 0:1]
    pre = pre_ref[...]
    out_ref[...] = pre
    sol_ref[...] = alpha * pre
    res_ref[...] = rhs_ref[...] - alpha * image_ref[...]


def body(land_sea, obs_cell, obs_value, obs_weight, intersection, factors, coarse_inverse):
    n_lat, n_lon = lax.axis_size("lat"), lax.axis_size("lon")
    cy, cx = land_sea.shape
    h, w = cy + 2 * HW, cx + 2 * HW
    others = n_lat * n_lon - 1
    sums = others if others < DIRECT else n_lon - 1
    copies = 2 * (n_lat - 1) + n_lon - 1 + sums + 16
    vmem = pl.BlockSpec(memory_space=pltpu.VMEM)
    entries = SUB * SUB
    lines = n_lat // min(n_lat, LANES // entries)
    hbm = pl.BlockSpec(memory_space=pltpu.HBM)
    out = jax.ShapeDtypeStruct((cx, cy), F32)
    fields = pl.pallas_call(
        functools.partial(kernel, n_lat, n_lon),
        out_shape=(out, out, out, jax.ShapeDtypeStruct((8, LANES), F32)),
        in_specs=[hbm, hbm, hbm, hbm, pl.BlockSpec(memory_space=pltpu.SMEM), hbm, hbm],
        out_specs=(hbm, hbm, hbm, vmem),
        scratch_shapes=[
            pltpu.VMEM((cx, cy), jnp.int32),
            pltpu.VMEM(obs_cell.shape, jnp.int32),
            pltpu.VMEM(obs_value.shape, F32),
            pltpu.VMEM(obs_weight.shape, F32),
            pltpu.VMEM(factors.shape, F32),
            pltpu.VMEM(coarse_inverse.shape, F32),
            pltpu.VMEM((cy, w), F32),
            pltpu.VMEM((2, cy, w), F32),
            pltpu.VMEM((2, h, w), F32),
            pltpu.VMEM((2, cy // 4, LANES), F32),
            pltpu.VMEM((2, cy // 4, LANES), F32),
            pltpu.VMEM((4, HW, LANES), F32),
            pltpu.VMEM((2, 2, HW, w), F32),
            pltpu.VMEM((4, HW, LANES), F32),
            pltpu.VMEM((n_lat, 1, LANES), F32),
            pltpu.VMEM((n_lon, lines, 1, LANES), F32),
            pltpu.VMEM((h, w), F32),
            pltpu.VMEM((2, h // 4, LANES), F32),
            pltpu.VMEM((2, h // 4, LANES), F32),
            pltpu.VMEM((2, 2 * HW, w), F32),
            pltpu.VMEM((4, HW // 2, LANES), F32),
            pltpu.VMEM((4, HW // 2, LANES), F32),
            pltpu.VMEM((h, w), F32),
            pltpu.VMEM((2, LANES), F32),
            pltpu.VMEM((n_lat - 1, 2, LANES), F32),
            pltpu.VMEM((2, LANES), F32),
            pltpu.VMEM((sums, 2, LANES), F32),
            pltpu.VMEM((3, cx, cy), F32),
            pltpu.SemaphoreType.DMA((6,)),
            pltpu.SemaphoreType.DMA((3,)),
            pltpu.SemaphoreType.DMA((copies,)),
            pltpu.SemaphoreType.DMA((copies,)),
        ],
        compiler_params=pltpu.CompilerParams(
            collective_id=0, has_side_effects=True, vmem_limit_bytes=64 * 1024 * 1024
        ),
    )(land_sea.T, obs_cell, obs_value, obs_weight, intersection, factors, coarse_inverse)
    results = pl.pallas_call(
        finish,
        out_shape=(out, out, out),
        in_specs=[vmem] * 4,
        out_specs=(vmem, vmem, vmem),
        compiler_params=pltpu.CompilerParams(vmem_limit_bytes=64 * 1024 * 1024),
    )(*fields)
    return tuple(x.T for x in results)


def solution(mesh):
    in_specs = (
        P("lat", "lon"),
        P("lat", "lon", None),
        P("lat", "lon", None),
        P("lat", "lon", None),
        P("lat", "lon"),
        P("lat", None, None, "lon"),
        P(("lon", "lat"), None),
    )
    out_specs = (P("lat", "lon"), P("lat", "lon"), P("lat", "lon"))
    return jax.shard_map(body, mesh=mesh, in_specs=in_specs, out_specs=out_specs, check_vma=False)
```
